128 devices in a mesh: dom: 16 (over z, y), sub: 8 (over x, core).
Axes of the slice: x: 4, y: 4, z: 4, core: 2. Of those that a mesh axis runs over, the one named last changes fastest.
Arguments:
- embeddings: float32 [262144, 400], P(('dom', 'sub')), may hold values from -5 to 5
- adagrad_state: float32 [262144], P(('dom', 'sub')), may hold values from 0.01 to 0.1
- relations: float32 [7424, 400], replicated, may hold values from 0.5 to 2
- pairing: int32 [2], replicated, may hold values from 1 to 15, as said below
- row_lists: int32 [2, 32768], P(None, ('dom', 'sub')), may hold values from 0 to 2047, as said below
- row_counts: int32 [2, 128], P(None, ('dom', 'sub')), may hold values from 1 to 256, as said below
- group_counts: int32 [2, 128], P(None, ('dom', 'sub')), may hold values from 1 to 3, as said below
- head_ids: int32 [2, 384000], P(None, ('dom', 'sub')), may hold values from 0 to 2047
- relation_ids: int32 [2, 384000], P(None, ('dom', 'sub')), may hold values from 0 to 7423
- tail_slots: int32 [2, 384000], P(None, ('dom', 'sub')), may hold values from 0 to 2047, as said below
- negatives: int32 [2, 384000], P(None, ('dom', 'sub')), may hold values from 0 to 2047, as said below
Outputs:
- new_embeddings: float32 [262144, 400], P(('dom', 'sub'))
- new_state: float32 [262144], P(('dom', 'sub'))
The draws below stay inside these ranges and needn't reach their ends.
Inputs may be any that keep to these rules, and one draw needn't show every extreme that they name: pairing[r] is the partner mask of round r; in some round it is 16 - 1. `row_lists`: the entries of one device's list in one round are distinct local row ids; entries from slot row_counts on are ignored. `row_counts`: in each round some device's list is full. `group_counts`: in each round some device uses all 3 edge group slots. `tail_slots`: A slot s' * 256 + k names slot k of the list of the partner device with sub index s', and k is below that list's count in that round. `negatives`: as for tail_slots.
All inputs are finite; a program needn't handle non-finite values.
Results may differ from the reference program's by a relative error of at most 0.0003.
Values sent between devices are 32-bit elements; how exact they have to be, the bound alone decides.
A program may use at most 192 MiB of HBM per device.

```python
import math
import jax
import jax.numpy as jnp
from jax import lax

D = 400
NREL = 7424
ROWS_DEV = 2048
LIST = 256
GROUP = 1000
NNEG = 1000
GROUPS_DEV = 3
ROUNDS = 2
ENTITIES = 262144
N_DOM = 16
N_SUB = 8


def plan(key):
    device_total = N_DOM * N_SUB
    random_masks = jax.random.randint(jax.random.fold_in(key, 100), (ROUNDS,), 1, N_DOM, dtype=jnp.int32)
    widest_round = jax.random.randint(jax.random.fold_in(key, 103), (), 0, ROUNDS, dtype=jnp.int32)
    pairing = jnp.where(jnp.arange(ROUNDS, dtype=jnp.int32) == widest_round, N_DOM - 1, random_masks).astype(jnp.int32)
    base = jax.random.randint(jax.random.fold_in(key, 101), (ROUNDS, device_total), LIST // 4, LIST + 1, dtype=jnp.int32)
    fullest = jax.random.randint(jax.random.fold_in(key, 102), (ROUNDS, 1), 0, device_total, dtype=jnp.int32)
    counts = jnp.where(jnp.arange(device_total, dtype=jnp.int32)[None, :] == fullest, LIST, base)
    return (pairing, counts.astype(jnp.int32))


def valid_slots(key, slot_key, per_device):
    pairing, counts = plan(key)
    device_total = N_DOM * N_SUB
    length = device_total * per_device
    owner_device = jnp.arange(length, dtype=jnp.int32) // per_device
    partner_dom = jnp.bitwise_xor(owner_device[None, :] // N_SUB, pairing[:, None])
    sub_pick = jax.random.randint(jax.random.fold_in(slot_key, 1), (ROUNDS, length), 0, N_SUB, dtype=jnp.int32)
    limit = jnp.take_along_axis(counts, partner_dom * N_SUB + sub_pick, axis=1)
    offset = jax.random.randint(jax.random.fold_in(slot_key, 2), (ROUNDS, length), 0, limit, dtype=jnp.int32)
    return (sub_pick * LIST + offset).astype(jnp.int32)


def draw_pairing(key, part):
    pairing, counts = plan(key)
    return pairing


def draw_row_counts(key, part):
    pairing, counts = plan(key)
    return counts


def draw_tail_slots(key, part):
    return valid_slots(key, jax.random.fold_in(key, 7), GROUPS_DEV * GROUP)


def draw_negatives(key, part):
    return valid_slots(key, jax.random.fold_in(key, 8), GROUPS_DEV * NNEG)


def draw_row_lists(key, part):
    key = jax.random.fold_in(key, 5)
    device_total = N_DOM * N_SUB
    keys = jax.random.split(key, ROUNDS * device_total)
    chosen = jax.vmap(lambda single_key: jax.random.permutation(single_key, ROWS_DEV)[:LIST])(keys)
    return chosen.reshape(ROUNDS, device_total * LIST).astype(jnp.int32)


def draw_group_counts(key, part):
    key = jax.random.fold_in(key, 6)
    device_total = N_DOM * N_SUB
    base = jax.random.randint(jax.random.fold_in(key, 1), (ROUNDS, device_total), 1, GROUPS_DEV + 1, dtype=jnp.int32)
    fullest = jax.random.randint(jax.random.fold_in(key, 2), (ROUNDS, 1), 0, device_total, dtype=jnp.int32)
    return jnp.where(jnp.arange(device_total, dtype=jnp.int32)[None, :] == fullest, GROUPS_DEV, base).astype(jnp.int32)


def draw_embeddings(key, part):
    key = jax.random.fold_in(key, 9)
    total_rows = ROWS_DEV * N_DOM * N_SUB
    values = jnp.clip(0.3 * jax.random.normal(jax.random.fold_in(key, 3), (total_rows, D), jnp.float32), -1.8, 1.8)
    return values.astype(jnp.float32)


def set_ends(result, own_key, least, high):
    longest = result.shape.index(max(result.shape))
    spots = []
    for shift in (0, 1):
        where = [jax.random.randint(jax.random.fold_in(own_key, axis), (), 0, length) for axis, length in enumerate(result.shape)]
        where[longest] = (where[longest] + shift) % result.shape[longest]
        spots.append(tuple(where))
    return result.at[spots[0]].set(least).at[spots[1]].set(high)


def steps_of(own_key, extent, cuts, least, largest):
    def one(axis_at, blocks):
        steps = jax.random.uniform(jax.random.fold_in(jax.random.fold_in(own_key, 6), axis_at), (blocks,), jnp.float32, least / len(cuts), largest / len(cuts))
        return jnp.repeat(jnp.exp(steps), extent[axis_at] // blocks).reshape((-1,) + (1,) * (len(extent) - axis_at - 1))

    loudness = one(*cuts[0])
    for cut in cuts[1:]:
        loudness = loudness * one(*cut)
    return loudness


def setup_inputs(seed: int = 0) -> dict:
    key_list = jax.random.split(jax.random.key(seed), 12)
    return {
        "embeddings": draw_embeddings(jax.random.fold_in(key_list[11], 71), 0),
        "adagrad_state": jnp.clip(jnp.exp(math.log(0.1) - 2.3025851 * jax.random.uniform(key_list[1], (ENTITIES,), jnp.float32) ** steps_of(key_list[1], (ENTITIES,), ((0, 128),), -0.2, 0.2)), 0.01, 0.1),
        "relations": jnp.clip(jax.random.uniform(key_list[2], (NREL, D), jnp.float32, 0.5, 2.0), 0.5, 2.0),
        "pairing": draw_pairing(jax.random.fold_in(key_list[11], 71), 0),
        "row_lists": draw_row_lists(jax.random.fold_in(key_list[11], 71), 0),
        "row_counts": draw_row_counts(jax.random.fold_in(key_list[11], 71), 0),
        "group_counts": draw_group_counts(jax.random.fold_in(key_list[11], 71), 0),
        "head_ids": set_ends(jax.random.randint(key_list[7], (ROUNDS, N_DOM * N_SUB * GROUPS_DEV * GROUP), 0, ROWS_DEV), jax.random.fold_in(key_list[7], 1), 0, ROWS_DEV - 1).astype(jnp.int32),
        "relation_ids": set_ends(jax.random.randint(key_list[8], (ROUNDS, N_DOM * N_SUB * GROUPS_DEV * GROUP), 0, NREL), jax.random.fold_in(key_list[8], 1), 0, NREL - 1).astype(jnp.int32),
        "tail_slots": draw_tail_slots(jax.random.fold_in(key_list[11], 71), 0),
        "negatives": draw_negatives(jax.random.fold_in(key_list[11], 71), 0),
    }


exact_mode = lax.Precision.HIGHEST
learn_rate = 0.1

def group_terms(own_rows, partner_block, relations, head_part, relation_part, tail_part, negative_part, active):
    head_rows = own_rows[head_part]
    scale_rows = relations[relation_part]
    queries = head_rows * scale_rows
    tail_rows = partner_block[tail_part]
    negative_rows = partner_block[negative_part]
    positive = lax.optimization_barrier(jnp.sum(queries * tail_rows, axis=1))
    negative = jnp.dot(queries, negative_rows.T, precision=exact_mode, preferred_element_type=jnp.float32)
    highest = jnp.maximum(lax.optimization_barrier(jnp.max(negative, axis=1)), positive)
    pos_weight = jnp.exp(positive - highest)
    neg_weight = jnp.exp(negative - highest[:, None])
    totals = pos_weight + lax.optimization_barrier(jnp.sum(neg_weight, axis=1))
    pos_share = pos_weight / totals * active - active
    neg_share = neg_weight / totals[:, None] * active
    query_grad = pos_share[:, None] * tail_rows + jnp.dot(neg_share, negative_rows, precision=exact_mode, preferred_element_type=jnp.float32)
    negative_grad = jnp.dot(neg_share.T, queries, precision=exact_mode, preferred_element_type=jnp.float32)
    return (query_grad * scale_rows, pos_share[:, None] * queries, negative_grad)

def device_round(own_rows, partner_block, relations, head_all, relation_all, tail_all, negative_all, group_total):
    rows_grad = jnp.zeros((ROWS_DEV, D), jnp.float32)
    block_grad = jnp.zeros((N_SUB * LIST, D), jnp.float32)

    def step(group_index, sums_carry):
        rows_grad, block_grad = sums_carry
        first = group_index * GROUP
        head_part = lax.dynamic_slice_in_dim(head_all, first, GROUP)
        relation_part = lax.dynamic_slice_in_dim(relation_all, first, GROUP)
        tail_part = lax.dynamic_slice_in_dim(tail_all, first, GROUP)
        negative_part = lax.dynamic_slice_in_dim(negative_all, group_index * NNEG, NNEG)
        active = (group_index < group_total).astype(jnp.float32)
        head_grad, tail_grad, negative_grad = group_terms(own_rows, partner_block, relations, head_part, relation_part, tail_part, negative_part, active)
        rows_grad = rows_grad.at[head_part].add(head_grad)
        block_grad = block_grad.at[tail_part].add(tail_grad).at[negative_part].add(negative_grad)
        return (rows_grad, block_grad)
    return lax.fori_loop(0, GROUPS_DEV, step, (rows_grad, block_grad))

def reference(embeddings, adagrad_state, relations, pairing, row_lists, row_counts, group_counts, head_ids, relation_ids, tail_slots, negatives):
    device_total = N_DOM * N_SUB
    table = embeddings.reshape(device_total, ROWS_DEV, D)
    state = adagrad_state.reshape(device_total, ROWS_DEV)
    for round_number in range(ROUNDS):
        lists = row_lists[round_number].reshape(device_total, LIST)
        filled = jnp.arange(LIST, dtype=jnp.int32)[None, :] < row_counts[round_number][:, None]
        picked = jax.vmap(lambda rows, where_rows: rows[where_rows])(table, lists)
        sent = jnp.where(filled[:, :, None], picked, 0.0)
        partners = jnp.bitwise_xor(jnp.arange(N_DOM, dtype=jnp.int32), pairing[round_number])
        blocks = sent.reshape(N_DOM, N_SUB * LIST, D)[partners]

        def per_device(inputs):
            device_index, own_rows, head_all, relation_all, tail_all, negative_all, group_total = inputs
            return device_round(own_rows, blocks[device_index // N_SUB], relations, head_all, relation_all, tail_all, negative_all, group_total)
        rows_grads, block_grads = lax.map(per_device, (jnp.arange(device_total, dtype=jnp.int32), table, head_ids[round_number].reshape(device_total, GROUPS_DEV * GROUP), relation_ids[round_number].reshape(device_total, GROUPS_DEV * GROUP), tail_slots[round_number].reshape(device_total, GROUPS_DEV * GROUP), negatives[round_number].reshape(device_total, GROUPS_DEV * NNEG), group_counts[round_number]))
        summed = lax.optimization_barrier(jnp.sum(block_grads.reshape(N_DOM, N_SUB, N_SUB, LIST, D), axis=1))
        returned = summed[partners].reshape(device_total, LIST, D)
        returned = jnp.where(filled[:, :, None], returned, 0.0)
        totals = jax.vmap(lambda grads, where_rows, extra: grads.at[where_rows].add(extra))(rows_grads, lists, returned)
        state = state + lax.optimization_barrier(jnp.mean(totals * totals, axis=2))
        table = table - learn_rate * totals / jnp.sqrt(state)[:, :, None]
    return (table.reshape(ENTITIES, D), state.reshape(ENTITIES))
```

```python
import jax
import jax.numpy as jnp
from jax import lax
from jax.experimental import pallas as pl
from jax.experimental.pallas import tpu as pltpu
from jax.sharding import PartitionSpec as P

F32 = jnp.float32
BF16 = jnp.bfloat16
LOG2E = 1.4426950408889634
LEARN_RATE = 0.1

D = 400
FULL = 384
TAIL = D - FULL
GROUP = 1000
GPAD = 1024
LIST = 256
SUBS = 8
SLOTS = SUBS * LIST
KCAT = 3 * FULL + 128
VMEM_LIMIT = 60 * 1024 * 1024

VSPEC = pl.BlockSpec(memory_space=pltpu.VMEM)
SSPEC = pl.BlockSpec(memory_space=pltpu.SMEM)


def split2(x):
    high = x.astype(BF16)
    return high, (x - high.astype(F32)).astype(BF16)


def split3(x):
    high, rest = split2(x)
    low = x - high.astype(F32) - rest.astype(F32)
    return high, rest, low.astype(BF16)


def dot(a, b):
    return lax.dot_general(a, b, (((1,), (0,)), ((), ())), preferred_element_type=F32)


def dot_nt(a, b):
    return lax.dot_general(a, b, (((1,), (1,)), ((), ())), preferred_element_type=F32)


def params(**more):
    return pltpu.CompilerParams(vmem_limit_bytes=VMEM_LIMIT, **more)


def cost(flops, moved):
    return pl.CostEstimate(flops=int(flops), bytes_accessed=int(moved), transcendentals=0)


def pack_rows(source, target, start, target_start):
    for j in range(4):
        if j < 3:
            tile = source[128 * j : 128 * (j + 1), pl.ds(start, 128)]
        else:
            tile = jnp.concatenate(
                [source[FULL:D, pl.ds(start, 128)], jnp.zeros((128 - TAIL, 128), F32)], axis=0
            )
        target[pl.ds(target_start + j, 128, stride=4), :] = tile.T


def relation_kernel(ids, table_t, out, packed):
    half = table_t.shape[1]
    step = pl.program_id(0)
    first = step * half

    @pl.loop(0, half // 128)
    def _(i):
        start = pl.multiple_of(i * 128, 128)
        pack_rows(table_t, packed, start, (first + start) * 4)

    @pl.when(step == pl.num_programs(0) - 1)
    def _():
        rounds, edges = ids.shape

        for r in range(rounds):

            @pl.loop(0, edges // 8)
            def _(i):
                for u in range(8):
                    e = i * 8 + u
                    row = pl.multiple_of(ids[r, e] * 4, 4)
                    at = pl.multiple_of(e * 4, 4)
                    out[r, pl.ds(at, 4), :] = packed[pl.ds(row, 4), :]


def gather_relations(relation_ids, relations_t):
    rounds, edges = relation_ids.shape
    count = relations_t.shape[1]
    half = count // 2
    return pl.pallas_call(
        relation_kernel,
        grid=(2,),
        in_specs=[SSPEC, pl.BlockSpec((D, half), lambda i: (0, i))],
        out_specs=pl.BlockSpec((rounds, edges * 4, 128), lambda i: (0, 0, 0)),
        out_shape=jax.ShapeDtypeStruct((rounds, edges * 4, 128), F32),
        scratch_shapes=[pltpu.VMEM((count * 4, 128), F32)],
        compiler_params=params(),
        cost_estimate=cost(2e9, 60e6),
        name="relation_rows",
    )(relation_ids, relations_t)


def pick_columns(table_t, ids_row, count):
    rows = table_t.shape[1]
    slot = lax.broadcasted_iota(jnp.int32, ids_row.shape, 1)
    wanted = jnp.where(slot < count, ids_row, -1)
    row = lax.broadcasted_iota(jnp.int32, (rows, LIST), 0)
    onehot = jnp.where(row == wanted, 1.0, 0.0).astype(BF16)
    high, mid, low = split3(table_t)
    return dot(high, onehot) + dot(mid, onehot) + dot(low, onehot)


def sent_kernel(counts, ids, table_t, out):
    out[...] = pick_columns(table_t[...], ids[0:1, :], counts[0, 0])


def first_sent(row_counts, row_lists, table_t):
    return pl.pallas_call(
        sent_kernel,
        in_specs=[SSPEC, VSPEC, VSPEC],
        out_specs=VSPEC,
        out_shape=jax.ShapeDtypeStruct((D, LIST), F32),
        compiler_params=params(),
        name="sent_rows",
    )(row_counts, row_lists, table_t)


def query_kernel(round_number, ids, table_t, scale, cat, flipped, table, packed):
    groups = cat.shape[0]

    @pl.loop(0, table_t.shape[1] // 128)
    def _(i):
        start = pl.multiple_of(i * 128, 128)
        pack_rows(table_t, table, start, start * 4)

    for g in range(groups):

        @pl.loop(0, GROUP // 8)
        def _(i):
            for u in range(8):
                e = i * 8 + u
                row = pl.multiple_of(ids[round_number, g * GROUP + e] * 4, 4)
                at = pl.multiple_of(e * 4, 4)
                scaled = pl.multiple_of((g * GROUP + e) * 4, 4)
                packed[pl.ds(at, 4), :] = table[pl.ds(row, 4), :] * scale[0, pl.ds(scaled, 4), :]

        packed[4 * GROUP :, :] = jnp.zeros((4 * (GPAD - GROUP), 128), F32)

        @pl.loop(0, GPAD // 128)
        def _(b):
            rows = pl.ds(pl.multiple_of(b * 128, 128), 128)
            for j in range(4):
                tile = packed[pl.ds(b * 512 + j, 128, stride=4), :]
                high, low = split2(tile * LOG2E)
                if j < 3:
                    cat[g, rows, 128 * j : 128 * (j + 1)] = high
                    cat[g, rows, FULL + 128 * j : FULL + 128 * (j + 1)] = high
                    cat[g, rows, 2 * FULL + 128 * j : 2 * FULL + 128 * (j + 1)] = low
                else:
                    high, low = high.astype(F32), low.astype(F32)
                    both = high + pltpu.roll(high, TAIL, 1) + pltpu.roll(low, 2 * TAIL, 1)
                    cat[g, rows, 3 * FULL :] = both.astype(BF16)
                high, low = split2(tile.T)
                width = 128 if j < 3 else TAIL
                flipped[g, 128 * j : 128 * j + width, rows] = high[:width]
                flipped[g, D + 128 * j : D + 128 * j + width, rows] = low[:width]


def make_queries(round_number, head_ids, table_t, scale, groups):
    def kernel(*refs):
        query_kernel(round_number, *refs)

    edges = scale.shape[1]
    return pl.pallas_call(
        kernel,
        grid=(1,),
        in_specs=[SSPEC, VSPEC, pl.BlockSpec((1, edges, 128), lambda i: (round_number, 0, 0))],
        out_specs=[VSPEC, VSPEC],
        out_shape=[
            jax.ShapeDtypeStruct((groups, GPAD, KCAT), BF16),
            jax.ShapeDtypeStruct((groups, 2 * D, GPAD), BF16),
        ],
        scratch_shapes=[
            pltpu.VMEM((table_t.shape[1] * 4, 128), F32),
            pltpu.VMEM((GPAD * 4, 128), F32),
        ],
        compiler_params=params(),
        cost_estimate=cost(2e9, 40e6),
        name="queries",
    )(head_ids, table_t, scale)


def score_kernel(
    round_number, counts, cat, flipped, block, tails, negatives, share, block_grad,
    block_cat, scores, tail_columns, bias,
):
    g = pl.program_id(0)

    @pl.when(g == 0)
    def _():
        @pl.loop(0, SUBS)
        def _(s):
            high, low = split2(block[s])
            block_cat[s, 0:FULL, :] = high[:FULL]
            block_cat[s, FULL : 2 * FULL, :] = low[:FULL]
            block_cat[s, 2 * FULL : 3 * FULL, :] = high[:FULL]
            block_cat[s, 3 * FULL : 3 * FULL + TAIL, :] = high[FULL:]
            block_cat[s, 3 * FULL + TAIL : 3 * FULL + 2 * TAIL, :] = low[FULL:]
            block_cat[s, 3 * FULL + 2 * TAIL : 3 * FULL + 3 * TAIL, :] = high[FULL:]
            block_cat[s, 3 * FULL + 3 * TAIL :, :] = jnp.zeros((128 - 3 * TAIL, LIST), BF16)
            block_grad[s] = jnp.zeros((D, LIST), F32)

    @pl.when(g < counts[round_number, 0])
    def _():
        @pl.loop(0, SUBS)
        def _(s):
            at = pl.ds(pl.multiple_of(s * LIST, LIST), LIST)
            scores[:, at] = dot(cat[0], block_cat[s])

        drawn = negatives[0, 0]
        total = jnp.zeros((16, 128), F32)
        low_iota = lax.broadcasted_iota(jnp.int32, (128, 128), 0)
        high_iota = lax.broadcasted_iota(jnp.int32, (16, 128), 0)
        for b in range(GPAD // 128):
            row = drawn[b : b + 1, :]
            low_hot = jnp.where(low_iota == jnp.bitwise_and(row, 127), 1.0, 0.0).astype(BF16)
            high_hot = jnp.where(high_iota == jnp.right_shift(row, 7), 1.0, 0.0).astype(BF16)
            total = total + dot_nt(high_hot, low_hot)
        bias[...] = jnp.where(total > 0.5, jnp.log2(jnp.maximum(total, 1.0)), -1e30)

        tail = tails[0, 0].astype(F32)
        for b in range(GPAD // 128):
            tail_columns[128 * b : 128 * (b + 1), :] = jnp.broadcast_to(tail[b : b + 1, :], (128, 128)).T

        rows_here = 16
        lane = lax.broadcasted_iota(jnp.int32, (rows_here, 128), 1).astype(F32)
        row_iota = lax.broadcasted_iota(jnp.int32, (rows_here, 1), 0)
        tiles = SLOTS // 128

        @pl.loop(0, GPAD // rows_here, unroll=2)
        def _(i):
            first = pl.multiple_of(i * rows_here, rows_here)
            rows = pl.ds(first, rows_here)
            offset = tail_columns[rows, :] - lane
            own = None
            shifted = []
            top = None
            for j in range(tiles):
                raw = scores[rows, 128 * j : 128 * (j + 1)]
                hit = jnp.where(offset == 128.0 * j, raw, 0.0)
                own = hit if own is None else own + hit
                moved = raw + bias[j : j + 1, :]
                shifted.append(moved)
                top = moved if top is None else jnp.maximum(top, moved)
            positive = jnp.sum(own, axis=1, keepdims=True)
            top = jnp.maximum(jnp.max(top, axis=1, keepdims=True), positive)
            total = None
            weights = []
            for j in range(tiles):
                weight = jnp.exp2(shifted[j] - top)
                weights.append(weight)
                total = weight if total is None else total + weight
            negative_sum = jnp.sum(total, axis=1, keepdims=True)
            active = jnp.where(row_iota + first < GROUP, 1.0, 0.0)
            inverse = active / (jnp.exp2(positive - top) + negative_sum)
            own_share = -negative_sum * inverse
            for j in range(tiles):
                value = weights[j] * inverse + jnp.where(offset == 128.0 * j, own_share, 0.0)
                high, low = split2(value)
                share[0, 0, rows, 128 * j : 128 * (j + 1)] = high
                share[0, 1, rows, 128 * j : 128 * (j + 1)] = low

        @pl.loop(0, SUBS)
        def _(s):
            at = pl.ds(pl.multiple_of(s * LIST, LIST), LIST)
            both = dot(flipped[0], share[0, 0, :, at])
            cross = dot(flipped[0, :D, :], share[0, 1, :, at])
            block_grad[s] += both[:D] + both[D:] + cross


def score_groups(round_number, group_counts, cat, flipped, block, tails, negatives):
    def kernel(*refs):
        score_kernel(round_number, *refs)

    groups = cat.shape[0]
    return pl.pallas_call(
        kernel,
        grid=(groups,),
        in_specs=[
            SSPEC,
            pl.BlockSpec((1, GPAD, KCAT), lambda g: (g, 0, 0)),
            pl.BlockSpec((1, 2 * D, GPAD), lambda g: (g, 0, 0)),
            VSPEC,
            pl.BlockSpec((1, 1, 8, 128), lambda g: (round_number, g, 0, 0)),
            pl.BlockSpec((1, 1, 8, 128), lambda g: (round_number, g, 0, 0)),
        ],
        out_specs=[pl.BlockSpec((1, 2, GPAD, SLOTS), lambda g: (g, 0, 0, 0)), VSPEC],
        out_shape=[
            jax.ShapeDtypeStruct((groups, 2, GPAD, SLOTS), BF16),
            jax.ShapeDtypeStruct((SUBS, D, LIST), F32),
        ],
        scratch_shapes=[
            pltpu.VMEM((SUBS, KCAT, LIST), BF16),
            pltpu.VMEM((GPAD, SLOTS), F32),
            pltpu.VMEM((GPAD, 128), F32),
            pltpu.VMEM((16, 128), F32),
        ],
        compiler_params=params(),
        cost_estimate=cost(40e9, 60e6),
        name="scores",
    )(group_counts, cat, flipped, block, tails, negatives)


def head_kernel(
    round_number, counts, ids, share, block, scale, out, rows_high, rows_low, grad, packed, *sums
):
    g = pl.program_id(0)
    parts = len(sums)

    @pl.when(g == 0)
    def _():
        @pl.loop(0, SUBS)
        def _(s):
            for h in range(LIST // 128):
                rows = pl.ds(pl.multiple_of(s * LIST + h * 128, 128), 128)
                for j in range(4):
                    if j < 3:
                        tile = block[s, 128 * j : 128 * (j + 1), 128 * h : 128 * (h + 1)]
                    else:
                        tile = jnp.concatenate(
                            [
                                block[s, FULL:D, 128 * h : 128 * (h + 1)],
                                jnp.zeros((128 - TAIL, 128), F32),
                            ],
                            axis=0,
                        )
                    high, low = split2(tile.T)
                    rows_high[rows, 128 * j : 128 * (j + 1)] = high
                    rows_low[rows, 128 * j : 128 * (j + 1)] = low

        for part in sums:
            part[...] = jnp.zeros_like(part)

    @pl.when(g < counts[round_number, 0])
    def _():
        for n in range(2):
            at = slice(256 * n, 256 * (n + 1))
            grad[...] = (
                dot(share[0, 0], rows_high[:, at])
                + dot(share[0, 0], rows_low[:, at])
                + dot(share[0, 1], rows_high[:, at])
            )
            for h in range(2):
                for b in range(GPAD // 128):
                    packed[pl.ds(512 * b + 2 * n + h, 128, stride=4), :] = grad[
                        128 * b : 128 * (b + 1), 128 * h : 128 * (h + 1)
                    ]

        base = g * GROUP

        @pl.loop(0, GROUP // parts, unroll=2)
        def _(i):
            news = []
            for u in range(parts):
                e = i * parts + u
                row = pl.ds(pl.multiple_of(ids[round_number, base + e] * 4, 4), 4)
                at = pl.ds(pl.multiple_of(e * 4, 4), 4)
                term = packed[at, :] * scale[0, at, :]
                news.append((row, sums[u][row, :] + term))
            for u in range(parts):
                row, value = news[u]
                sums[u][row, :] = value

    @pl.when(g == pl.num_programs(0) - 1)
    def _():
        @pl.loop(0, out.shape[1] // 128)
        def _(i):
            columns = pl.ds(pl.multiple_of(i * 128, 128), 128)
            for j in range(4):
                at = pl.ds(i * 512 + j, 128, stride=4)
                tile = sums[0][at, :]
                for part in sums[1:]:
                    tile = tile + part[at, :]
                width = 128 if j < 3 else TAIL
                out[128 * j : 128 * j + width, columns] = tile.T[:width]


def head_gradients(round_number, group_counts, head_ids, share, block, scale, rows):
    def kernel(*refs):
        head_kernel(round_number, *refs)

    groups = share.shape[0]
    parts = 4
    return pl.pallas_call(
        kernel,
        grid=(groups,),
        in_specs=[
            SSPEC,
            SSPEC,
            pl.BlockSpec((1, 2, GPAD, SLOTS), lambda g: (g, 0, 0, 0)),
            VSPEC,
            pl.BlockSpec((1, GROUP * 4, 128), lambda g: (round_number, g, 0)),
        ],
        out_specs=VSPEC,
        out_shape=jax.ShapeDtypeStruct((D, rows), F32),
        scratch_shapes=[
            pltpu.VMEM((SLOTS, 512), BF16),
            pltpu.VMEM((SLOTS, 512), BF16),
            pltpu.VMEM((GPAD, 256), F32),
            pltpu.VMEM((GPAD * 4, 128), F32),
        ]
        + [pltpu.VMEM((rows * 4, 128), F32)] * parts,
        compiler_params=params(),
        cost_estimate=cost(20e9, 60e6),
        name="head_gradients",
    )(group_counts, head_ids, share, block, scale)


def adagrad_kernel(
    round_number, last, counts, ids, ids_column, head_grad, returned, table_t, state,
    new_table_t, new_state, *sent,
):
    rows = table_t.shape[1]
    width = 512
    wanted = ids_column[round_number]
    slot = lax.broadcasted_iota(jnp.int32, wanted.shape, 0)
    wanted = jnp.where(slot < counts[round_number, 0], wanted, -1)
    high, mid, low = split3(returned[...])
    for first in range(0, rows, width):
        at = slice(first, first + width)
        row = lax.broadcasted_iota(jnp.int32, (LIST, width), 1) + first
        onehot = jnp.where(row == wanted, 1.0, 0.0).astype(BF16)
        totals = head_grad[:, at] + (dot(high, onehot) + dot(mid, onehot) + dot(low, onehot))
        fresh = state[:, at] + jnp.sum(totals * totals, axis=0, keepdims=True) / D
        new_state[:, at] = fresh
        new_table_t[:, at] = table_t[:, at] - LEARN_RATE * totals / jnp.sqrt(fresh)
    if not last:
        sent[0][...] = pick_columns(
            new_table_t[...], ids[round_number + 1 : round_number + 2, :], counts[round_number + 1, 0]
        )


def adagrad(round_number, last, row_counts, row_lists, ids_column, head_grad, returned, table_t, state):
    def kernel(*refs):
        adagrad_kernel(round_number, last, *refs)

    outs = [jax.ShapeDtypeStruct(table_t.shape, F32), jax.ShapeDtypeStruct(state.shape, F32)]
    if not last:
        outs.append(jax.ShapeDtypeStruct((D, LIST), F32))
    return pl.pallas_call(
        kernel,
        in_specs=[SSPEC] + [VSPEC] * 6,
        out_specs=[VSPEC] * len(outs),
        out_shape=outs,
        compiler_params=params(),
        name="adagrad",
    )(row_counts, row_lists, ids_column, head_grad, returned, table_t, state)


def swap_partner(values, mask):
    count = lax.axis_size("dom")

    def branch(m):
        route = [(i, i ^ m) for i in range(count)]
        return lambda held: lax.ppermute(held, "dom", route)

    return lax.switch(mask - 1, [branch(m) for m in range(1, count)], values)


def body(
    embeddings,
    adagrad_state,
    relations,
    pairing,
    row_lists,
    row_counts,
    group_counts,
    head_ids,
    relation_ids,
    tail_slots,
    negatives,
):
    rounds = pairing.shape[0]
    rows = embeddings.shape[0]
    groups = head_ids.shape[1] // GROUP
    table_t = embeddings.T
    state = adagrad_state.reshape(1, rows)
    ids_column = row_lists.reshape(rounds, LIST, 1)

    def lanes(ids):
        ids = ids.reshape(rounds, groups, GROUP)
        ids = jnp.pad(ids, ((0, 0), (0, 0), (0, GPAD - GROUP)), constant_values=-1)
        return ids.reshape(rounds, groups, GPAD // 128, 128)

    tails = lanes(tail_slots)
    drawn = lanes(negatives)
    sent = first_sent(row_counts, row_lists, table_t)
    scale = gather_relations(relation_ids, relations.T)
    for r in range(rounds):
        incoming = swap_partner(sent, pairing[r])
        block = lax.all_gather(incoming, "sub", axis=0, tiled=False)
        cat, flipped = make_queries(r, head_ids, table_t, scale, groups)
        share, block_grad = score_groups(r, group_counts, cat, flipped, block, tails, drawn)
        own_share = lax.psum_scatter(block_grad, "sub", scatter_dimension=0, tiled=False)
        head_grad = head_gradients(r, group_counts, head_ids, share, block, scale, rows)
        returned = swap_partner(own_share, pairing[r])
        last = r == rounds - 1
        done = adagrad(r, last, row_counts, row_lists, ids_column, head_grad, returned, table_t, state)
        table_t, state = done[0], done[1]
        if not last:
            sent = done[2]
    return (table_t.T, state.reshape(rows))


def solution(mesh):
    in_specs = (
        P(("dom", "sub"), None),
        P(("dom", "sub")),
        P(),
        P(),
        P(None, ("dom", "sub")),
        P(None, ("dom", "sub")),
        P(None, ("dom", "sub")),
        P(None, ("dom", "sub")),
        P(None, ("dom", "sub")),
        P(None, ("dom", "sub")),
        P(None, ("dom", "sub")),
    )
    out_specs = (P(("dom", "sub"), None), P(("dom", "sub")))
    return jax.shard_map(body, mesh=mesh, in_specs=in_specs, out_specs=out_specs, check_vma=False)
```

```python
import jax
import jax.numpy as jnp
from jax import lax
from jax.experimental import pallas as pl
from jax.experimental.pallas import tpu as pltpu
from jax.sharding import PartitionSpec as P

F32 = jnp.float32
BF16 = jnp.bfloat16
LOG2E = 1.4426950408889634
LEARN_RATE = 0.1

D = 400
FULL = 384
TAIL = D - FULL
GROUP = 1000
GPAD = 1024
LIST = 256
SUBS = 8
SLOTS = SUBS * LIST
STRIP = GPAD // 2
KCAT = 3 * FULL + 128
VMEM_LIMIT = 60 * 1024 * 1024

VSPEC = pl.BlockSpec(memory_space=pltpu.VMEM)
SSPEC = pl.BlockSpec(memory_space=pltpu.SMEM)


def split2(x):
    high = x.astype(BF16)
    return high, (x - high.astype(F32)).astype(BF16)


def split3(x):
    high, rest = split2(x)
    low = x - high.astype(F32) - rest.astype(F32)
    return high, rest, low.astype(BF16)


def dot(a, b):
    return lax.dot_general(a, b, (((1,), (0,)), ((), ())), preferred_element_type=F32)


def dot_nt(a, b):
    return lax.dot_general(a, b, (((1,), (1,)), ((), ())), preferred_element_type=F32)


def params(**more):
    return pltpu.CompilerParams(vmem_limit_bytes=VMEM_LIMIT, **more)


def cost(flops, moved):
    return pl.CostEstimate(flops=int(flops), bytes_accessed=int(moved), transcendentals=0)


def pack_rows(source, target, start, target_start):
    for j in range(4):
        if j < 3:
            tile = source[128 * j : 128 * (j + 1), pl.ds(start, 128)]
        else:
            tile = jnp.concatenate(
                [source[FULL:D, pl.ds(start, 128)], jnp.zeros((128 - TAIL, 128), F32)], axis=0
            )
        target[pl.ds(target_start + j, 128, stride=4), :] = tile.T


def relation_kernel(ids, table_t, out, packed):
    half = table_t.shape[1]
    step = pl.program_id(0)
    first = step * half

    @pl.loop(0, half // 128)
    def _(i):
        start = pl.multiple_of(i * 128, 128)
        pack_rows(table_t, packed, start, (first + start) * 4)

    @pl.when(step == pl.num_programs(0) - 1)
    def _():
        rounds, edges = ids.shape

        for r in range(rounds):

            @pl.loop(0, edges // 40)
            def _(i):
                for u in range(40):
                    e = i * 40 + u
                    row = pl.multiple_of(ids[r, e] * 4, 4)
                    at = pl.multiple_of(e * 4, 4)
                    out[r, pl.ds(at, 4), :] = packed[pl.ds(row, 4), :]


def gather_relations(relation_ids, relations_t):
    rounds, edges = relation_ids.shape
    count = relations_t.shape[1]
    half = count // 2
    return pl.pallas_call(
        relation_kernel,
        grid=(2,),
        in_specs=[SSPEC, pl.BlockSpec((D, half), lambda i: (0, i))],
        out_specs=pl.BlockSpec((rounds, edges * 4, 128), lambda i: (0, 0, 0)),
        out_shape=jax.ShapeDtypeStruct((rounds, edges * 4, 128), F32),
        scratch_shapes=[pltpu.VMEM((count * 4, 128), F32)],
        compiler_params=params(),
        cost_estimate=cost(2e9, 60e6),
        name="relation_rows",
    )(relation_ids, relations_t)


def pick_columns(table_t, ids_row, count):
    rows = table_t.shape[1]
    slot = lax.broadcasted_iota(jnp.int32, ids_row.shape, 1)
    wanted = jnp.where(slot < count, ids_row, -1)
    row = lax.broadcasted_iota(jnp.int32, (rows, LIST), 0)
    onehot = jnp.where(row == wanted, 1.0, 0.0).astype(BF16)
    high, mid, low = split3(table_t)
    return dot(high, onehot) + dot(mid, onehot) + dot(low, onehot)


def sent_kernel(counts, ids, table_t, out):
    out[...] = pick_columns(table_t[...], ids[0:1, :], counts[0, 0])


def first_sent(row_counts, row_lists, table_t):
    return pl.pallas_call(
        sent_kernel,
        in_specs=[SSPEC, VSPEC, VSPEC],
        out_specs=VSPEC,
        out_shape=jax.ShapeDtypeStruct((D, LIST), F32),
        compiler_params=params(),
        name="sent_rows",
    )(row_counts, row_lists, table_t)


def query_kernel(round_number, ids, table_t, scale, cat, flipped, table, packed):
    groups = cat.shape[0]

    @pl.loop(0, table_t.shape[1] // 128)
    def _(i):
        start = pl.multiple_of(i * 128, 128)
        pack_rows(table_t, table, start, start * 4)

    for g in range(groups):

        @pl.loop(0, GROUP // 40)
        def _(i):
            for u in range(40):
                e = i * 40 + u
                row = pl.multiple_of(ids[round_number, g * GROUP + e] * 4, 4)
                at = pl.multiple_of(e * 4, 4)
                scaled = pl.multiple_of((g * GROUP + e) * 4, 4)
                packed[pl.ds(at, 4), :] = table[pl.ds(row, 4), :] * scale[0, pl.ds(scaled, 4), :]

        packed[4 * GROUP :, :] = jnp.zeros((4 * (GPAD - GROUP), 128), F32)

        @pl.loop(0, GPAD // 128)
        def _(b):
            rows = pl.ds(pl.multiple_of(b * 128, 128), 128)
            for j in range(4):
                tile = packed[pl.ds(b * 512 + j, 128, stride=4), :]
                high, low = split2(tile * LOG2E)
                if j < 3:
                    cat[g, rows, 128 * j : 128 * (j + 1)] = high
                    cat[g, rows, FULL + 128 * j : FULL + 128 * (j + 1)] = high
                    cat[g, rows, 2 * FULL + 128 * j : 2 * FULL + 128 * (j + 1)] = low
                else:
                    high, low = high.astype(F32), low.astype(F32)
                    both = high + pltpu.roll(high, TAIL, 1) + pltpu.roll(low, 2 * TAIL, 1)
                    cat[g, rows, 3 * FULL :] = both.astype(BF16)
                high, low = split2(tile.T)
                width = 128 if j < 3 else TAIL
                flipped[g, 128 * j : 128 * j + width, rows] = high[:width]
                flipped[g, D + 128 * j : D + 128 * j + width, rows] = low[:width]


def make_queries(round_number, head_ids, table_t, scale, groups):
    def kernel(*refs):
        query_kernel(round_number, *refs)

    edges = scale.shape[1]
    return pl.pallas_call(
        kernel,
        grid=(1,),
        in_specs=[SSPEC, VSPEC, pl.BlockSpec((1, edges, 128), lambda i: (round_number, 0, 0))],
        out_specs=[VSPEC, VSPEC],
        out_shape=[
            jax.ShapeDtypeStruct((groups, GPAD, KCAT), BF16),
            jax.ShapeDtypeStruct((groups, 2 * D, GPAD), BF16),
        ],
        scratch_shapes=[
            pltpu.VMEM((table_t.shape[1] * 4, 128), F32),
            pltpu.VMEM((GPAD * 4, 128), F32),
        ],
        compiler_params=params(),
        cost_estimate=cost(2e9, 40e6),
        name="queries",
    )(head_ids, table_t, scale)


def softmax_rows(first, group, active_rows, active, scores, share_high, share_low, tail_columns, bias):
    count = 16
    rows = pl.ds(first, count)
    tiles = SLOTS // 128
    lane = lax.broadcasted_iota(jnp.int32, (count, 128), 1).astype(F32)
    offset = tail_columns[active_rows, :] - lane
    own = None
    shifted = []
    top = None
    for j in range(tiles):
        raw = scores[rows, 128 * j : 128 * (j + 1)]
        hit = jnp.where(offset == 128.0 * j, raw, 0.0)
        own = hit if own is None else own + hit
        moved = raw + bias[group, j : j + 1, :]
        shifted.append(moved)
        top = moved if top is None else jnp.maximum(top, moved)
    positive = jnp.sum(own, axis=1, keepdims=True)
    top = jnp.maximum(jnp.max(top, axis=1, keepdims=True), positive)
    total = None
    weights = []
    for j in range(tiles):
        weight = jnp.exp2(shifted[j] - top)
        weights.append(weight)
        total = weight if total is None else total + weight
    negative_sum = jnp.sum(total, axis=1, keepdims=True)
    inverse = active / (jnp.exp2(positive - top) + negative_sum)
    own_share = -negative_sum * inverse
    for j in range(tiles):
        value = weights[j] * inverse + jnp.where(offset == 128.0 * j, own_share, 0.0)
        high, low = split2(value)
        share_high[rows, 128 * j : 128 * (j + 1)] = high
        share_low[rows, 128 * j : 128 * (j + 1)] = low


def score_kernel(
    round_number, counts, cat_hbm, flipped_hbm, block, tails, negatives, share_hbm, block_grad,
    cat, flipped, block_cat, scores_a, scores_b, high_a, high_b, low_a, low_b, tail_columns, bias,
    in_sems, out_sems,
):
    groups = cat.shape[0]
    strips = groups * 2
    scores = (scores_a, scores_b)
    highs = (high_a, high_b)
    lows = (low_a, low_b)

    def load(g):
        return (
            pltpu.make_async_copy(cat_hbm.at[g], cat.at[g], in_sems.at[g, 0]),
            pltpu.make_async_copy(flipped_hbm.at[g], flipped.at[g], in_sems.at[g, 1]),
        )

    def store(t):
        target = pl.ds((t % 2) * STRIP, STRIP)
        return (
            pltpu.make_async_copy(highs[t % 2], share_hbm.at[t // 2, 0, target, :], out_sems.at[t % 2, 0]),
            pltpu.make_async_copy(lows[t % 2], share_hbm.at[t // 2, 1, target, :], out_sems.at[t % 2, 1]),
        )

    for g in range(groups):
        for copy in load(g):
            copy.start()

    @pl.loop(0, SUBS)
    def _(s):
        high, low = split2(block[s])
        block_cat[s, 0:FULL, :] = high[:FULL]
        block_cat[s, FULL : 2 * FULL, :] = low[:FULL]
        block_cat[s, 2 * FULL : 3 * FULL, :] = high[:FULL]
        block_cat[s, 3 * FULL : 3 * FULL + TAIL, :] = high[FULL:]
        block_cat[s, 3 * FULL + TAIL : 3 * FULL + 2 * TAIL, :] = low[FULL:]
        block_cat[s, 3 * FULL + 2 * TAIL : 3 * FULL + 3 * TAIL, :] = high[FULL:]
        block_cat[s, 3 * FULL + 3 * TAIL :, :] = jnp.zeros((128 - 3 * TAIL, LIST), BF16)
        block_grad[s] = jnp.zeros((D, LIST), F32)

    low_iota = lax.broadcasted_iota(jnp.int32, (128, 128), 0)
    high_iota = lax.broadcasted_iota(jnp.int32, (16, 128), 0)
    for g in range(groups):
        drawn = negatives[round_number, g]
        total = jnp.zeros((16, 128), F32)
        tail = tails[round_number, g].astype(F32)
        for b in range(GPAD // 128):
            row = drawn[b : b + 1, :]
            low_hot = jnp.where(low_iota == jnp.bitwise_and(row, 127), 1.0, 0.0).astype(BF16)
            high_hot = jnp.where(high_iota == jnp.right_shift(row, 7), 1.0, 0.0).astype(BF16)
            total = total + dot_nt(high_hot, low_hot)
            first = g * GPAD + 128 * b
            tail_columns[first : first + 128, :] = jnp.broadcast_to(tail[b : b + 1, :], (128, 128)).T
        bias[g] = jnp.where(total > 0.5, jnp.log2(jnp.maximum(total, 1.0)), -1e30)

    for stage in range(strips + 2):
        if stage < strips and stage % 2 == 0:
            for copy in load(stage // 2):
                copy.wait()
        if stage >= 3 and stage - 3 < strips - 2:
            for copy in store(stage - 3):
                copy.wait()

        @pl.loop(0, SUBS)
        def _(s):
            at = pl.ds(pl.multiple_of(s * LIST, LIST), LIST)
            if stage < strips:
                t = stage
                edges = slice((t % 2) * STRIP, (t % 2 + 1) * STRIP)
                scores[t % 2][:, at] = dot(cat[t // 2, edges, :], block_cat[s])
            if 2 <= stage:
                t = stage - 2
                edges = slice((t % 2) * STRIP, (t % 2 + 1) * STRIP)
                high = highs[t % 2][:, at]
                both = dot(flipped[t // 2, :, edges], high)
                cross = dot(flipped[t // 2, :D, edges], lows[t % 2][:, at])
                block_grad[s] += both[:D] + both[D:] + cross
            if 1 <= stage <= strips:
                t = stage - 1
                g = t // 2
                part = STRIP // SUBS
                row_iota = lax.broadcasted_iota(jnp.int32, (16, 1), 0)
                used = jnp.where(g < counts[round_number, 0], GROUP, 0)
                for u in range(part // 16):
                    first = pl.multiple_of(s * part + u * 16, 16)
                    in_group = first + (t % 2) * STRIP
                    softmax_rows(
                        first,
                        g,
                        pl.ds(pl.multiple_of(in_group + g * GPAD, 16), 16),
                        jnp.where(row_iota + in_group < used, 1.0, 0.0),
                        scores[t % 2],
                        highs[t % 2],
                        lows[t % 2],
                        tail_columns,
                        bias,
                    )

        if 1 <= stage <= strips:
            for copy in store(stage - 1):
                copy.start()

    for t in (strips - 2, strips - 1):
        for copy in store(t):
            copy.wait()


def score_groups(round_number, group_counts, cat, flipped, block, tails, negatives):
    def kernel(*refs):
        score_kernel(round_number, *refs)

    groups = cat.shape[0]
    anywhere = pl.BlockSpec(memory_space=pl.ANY)
    return pl.pallas_call(
        kernel,
        in_specs=[SSPEC, anywhere, anywhere, VSPEC, VSPEC, VSPEC],
        out_specs=[anywhere, VSPEC],
        out_shape=[
            jax.ShapeDtypeStruct((groups, 2, GPAD, SLOTS), BF16),
            jax.ShapeDtypeStruct((SUBS, D, LIST), F32),
        ],
        scratch_shapes=[
            pltpu.VMEM(cat.shape, BF16),
            pltpu.VMEM(flipped.shape, BF16),
            pltpu.VMEM((SUBS, KCAT, LIST), BF16),
            pltpu.VMEM((STRIP, SLOTS), F32),
            pltpu.VMEM((STRIP, SLOTS), F32),
            pltpu.VMEM((STRIP, SLOTS), BF16),
            pltpu.VMEM((STRIP, SLOTS), BF16),
            pltpu.VMEM((STRIP, SLOTS), BF16),
            pltpu.VMEM((STRIP, SLOTS), BF16),
            pltpu.VMEM((groups * GPAD, 128), F32),
            pltpu.VMEM((groups, 16, 128), F32),
            pltpu.SemaphoreType.DMA((groups, 2)),
            pltpu.SemaphoreType.DMA((2, 2)),
        ],
        compiler_params=params(),
        cost_estimate=cost(40e9, 60e6),
        name="scores",
    )(group_counts, cat, flipped, block, tails, negatives)


def reduce_kernel(
    share_hbm, block, block_grad, own_share, packed,
    rows_high, rows_low, parts, from_mate, sums, relay_ahead, relay_behind, from_left, from_right,
    load_sems, mate_send, mate_recv, ring_send, ring_recv,
):
    me = lax.axis_index("sub")
    x = me // 2
    core = me % 2
    chips = SUBS // 2
    mate = x * 2 + (1 - core)
    right = ((x + 1) % chips) * 2 + core
    left = ((x + chips - 1) % chips) * 2 + core
    half = D // 2
    upper, lower = pl.ds(0, half), pl.ds(half, half)
    groups = share_hbm.shape[0]
    strips = groups * 2

    def block_of(k, c):
        return ((x + k) % chips) * 2 + c

    def load(t):
        slot = t % 2
        return pltpu.make_async_copy(
            share_hbm.at[t // 2, :, pl.ds(pl.multiple_of(slot * STRIP, STRIP), STRIP), :],
            parts.at[slot],
            load_sems.at[slot],
        )

    def to(device, source, target, send, recv, n):
        return pltpu.make_async_remote_copy(
            src_ref=source,
            dst_ref=target,
            send_sem=send.at[n],
            recv_sem=recv.at[n],
            device_id={"sub": device},
            device_id_type=pl.DeviceIdType.MESH,
        )

    load(0).start()
    barrier = pltpu.get_barrier_semaphore()
    for other in (mate, right, left):
        pl.semaphore_signal(
            barrier, inc=1, device_id={"sub": other}, device_id_type=pl.DeviceIdType.MESH
        )
    pl.semaphore_wait(barrier, 3)

    mates = {
        k: to(mate, block_grad.at[block_of(k, 1 - core)], from_mate.at[k], mate_send, mate_recv, k)
        for k in range(chips)
    }
    for k in (2, 1, 3, 0):
        mates[k].start()
    ring = (
        to(right, sums.at[2, upper], relay_ahead, ring_send, ring_recv, 0),
        to(left, sums.at[2, lower], relay_behind, ring_send, ring_recv, 1),
        to(right, sums.at[1, lower], from_left.at[lower], ring_send, ring_recv, 2),
        to(left, sums.at[3, upper], from_right.at[upper], ring_send, ring_recv, 3),
        to(right, sums.at[1, upper], from_left.at[upper], ring_send, ring_recv, 4),
        to(left, sums.at[3, lower], from_right.at[lower], ring_send, ring_recv, 5),
    )

    @pl.loop(0, SUBS)
    def _(s):
        for h in range(LIST // 128):
            rows = pl.ds(pl.multiple_of(s * LIST + h * 128, 128), 128)
            for j in range(4):
                lanes = slice(128 * h, 128 * (h + 1))
                if j < 3:
                    tile = block[s, 128 * j : 128 * (j + 1), lanes]
                else:
                    tile = jnp.concatenate(
                        [block[s, FULL:D, lanes], jnp.zeros((128 - TAIL, 128), F32)], axis=0
                    )
                high, low = split2(tile.T)
                rows_high[rows, 128 * j : 128 * (j + 1)] = high
                rows_low[rows, 128 * j : 128 * (j + 1)] = low

    def query_strip(t, more):
        if more:
            load(t + 1).start()
        load(t).wait()
        slot = t % 2
        for n in range(2):
            at = slice(256 * n, 256 * (n + 1))
            grad = (
                dot(parts[slot, 0], rows_high[:, at])
                + dot(parts[slot, 0], rows_low[:, at])
                + dot(parts[slot, 1], rows_high[:, at])
            )
            for h in range(2):
                for b in range(STRIP // 128):
                    packed[pl.ds(t * (4 * STRIP) + 512 * b + 2 * n + h, 128, stride=4), :] = grad[
                        128 * b : 128 * (b + 1), 128 * h : 128 * (h + 1)
                    ]

    def pair_sum(k):
        mates[k].wait()
        sums[k] = block_grad[block_of(k, core)] + from_mate[k]

    pair_sum(2)
    ring[0].start()
    ring[1].start()
    pair_sum(1)
    ring[2].start()
    pair_sum(3)
    ring[3].start()
    pair_sum(0)

    @pl.loop(0, 2)
    def _(t):
        query_strip(t, True)

    ring[0].wait()
    sums[1, upper, :] += relay_ahead[...]
    ring[4].start()
    ring[1].wait()
    sums[3, lower, :] += relay_behind[...]
    ring[5].start()

    @pl.loop(2, strips - 1)
    def _(t):
        query_strip(t, True)

    query_strip(strips - 1, False)

    for n in (2, 3, 4, 5):
        ring[n].wait()
    own_share[...] = sums[0] + from_left[...] + from_right[...]


def reduce_block(share, block, block_grad):
    groups = share.shape[0]
    return pl.pallas_call(
        reduce_kernel,
        in_specs=[pl.BlockSpec(memory_space=pl.ANY), VSPEC, VSPEC],
        out_specs=[VSPEC, VSPEC],
        out_shape=[
            jax.ShapeDtypeStruct((D, LIST), F32),
            jax.ShapeDtypeStruct((groups * GPAD * 4, 128), F32),
        ],
        scratch_shapes=[
            pltpu.VMEM((SLOTS, 512), BF16),
            pltpu.VMEM((SLOTS, 512), BF16),
            pltpu.VMEM((2, 2, STRIP, SLOTS), BF16),
            pltpu.VMEM((SUBS // 2, D, LIST), F32),
            pltpu.VMEM((SUBS // 2, D, LIST), F32),
            pltpu.VMEM((D // 2, LIST), F32),
            pltpu.VMEM((D // 2, LIST), F32),
            pltpu.VMEM((D, LIST), F32),
            pltpu.VMEM((D, LIST), F32),
            pltpu.SemaphoreType.DMA((2,)),
            pltpu.SemaphoreType.DMA((4,)),
            pltpu.SemaphoreType.DMA((4,)),
            pltpu.SemaphoreType.DMA((6,)),
            pltpu.SemaphoreType.DMA((6,)),
        ],
        compiler_params=params(collective_id=0, has_side_effects=True),
        cost_estimate=cost(20e9, 60e6),
        name="reduce_block",
    )(share, block, block_grad)


def head_kernel(round_number, counts, ids, packed, scale, out, *sums):
    g = pl.program_id(0)
    parts = len(sums)

    @pl.when(g == 0)
    def _():
        for part in sums:
            part[...] = jnp.zeros_like(part)

    @pl.when(g < counts[round_number, 0])
    def _():
        base = g * GROUP

        @pl.loop(0, GROUP // parts, unroll=5)
        def _(i):
            news = []
            for u in range(parts):
                e = i * parts + u
                row = pl.ds(pl.multiple_of(ids[round_number, base + e] * 4, 4), 4)
                at = pl.ds(pl.multiple_of(e * 4, 4), 4)
                term = packed[at, :] * scale[0, at, :]
                news.append((row, sums[u][row, :] + term))
            for u in range(parts):
                row, value = news[u]
                sums[u][row, :] = value

    @pl.when(g == pl.num_programs(0) - 1)
    def _():
        @pl.loop(0, out.shape[1] // 128)
        def _(i):
            columns = pl.ds(pl.multiple_of(i * 128, 128), 128)
            for j in range(4):
                at = pl.ds(i * 512 + j, 128, stride=4)
                tile = sums[0][at, :]
                for part in sums[1:]:
                    tile = tile + part[at, :]
                width = 128 if j < 3 else TAIL
                out[128 * j : 128 * j + width, columns] = tile.T[:width]


def head_gradients(round_number, group_counts, head_ids, packed, scale, rows):
    def kernel(*refs):
        head_kernel(round_number, *refs)

    groups = packed.shape[0] // (GPAD * 4)
    parts = 4
    return pl.pallas_call(
        kernel,
        grid=(groups,),
        in_specs=[
            SSPEC,
            SSPEC,
            pl.BlockSpec((GPAD * 4, 128), lambda g: (g, 0)),
            pl.BlockSpec((1, GROUP * 4, 128), lambda g: (round_number, g, 0)),
        ],
        out_specs=VSPEC,
        out_shape=jax.ShapeDtypeStruct((D, rows), F32),
        scratch_shapes=[pltpu.VMEM((rows * 4, 128), F32)] * parts,
        compiler_params=params(),
        cost_estimate=cost(2e9, 40e6),
        name="head_gradients",
    )(group_counts, head_ids, packed, scale)


def adagrad_kernel(
    round_number, last, counts, ids, ids_column, head_grad, returned, table_t, state,
    new_table_t, new_state, *sent,
):
    rows = table_t.shape[1]
    width = 512
    wanted = ids_column[round_number]
    slot = lax.broadcasted_iota(jnp.int32, wanted.shape, 0)
    wanted = jnp.where(slot < counts[round_number, 0], wanted, -1)
    high, mid, low = split3(returned[...])
    for first in range(0, rows, width):
        at = slice(first, first + width)
        row = lax.broadcasted_iota(jnp.int32, (LIST, width), 1) + first
        onehot = jnp.where(row == wanted, 1.0, 0.0).astype(BF16)
        totals = head_grad[:, at] + (dot(high, onehot) + dot(mid, onehot) + dot(low, onehot))
        fresh = state[:, at] + jnp.sum(totals * totals, axis=0, keepdims=True) / D
        new_state[:, at] = fresh
        new_table_t[:, at] = table_t[:, at] - LEARN_RATE * totals / jnp.sqrt(fresh)
    if not last:
        sent[0][...] = pick_columns(
            new_table_t[...], ids[round_number + 1 : round_number + 2, :], counts[round_number + 1, 0]
        )


def adagrad(round_number, last, row_counts, row_lists, ids_column, head_grad, returned, table_t, state):
    def kernel(*refs):
        adagrad_kernel(round_number, last, *refs)

    outs = [jax.ShapeDtypeStruct(table_t.shape, F32), jax.ShapeDtypeStruct(state.shape, F32)]
    if not last:
        outs.append(jax.ShapeDtypeStruct((D, LIST), F32))
    return pl.pallas_call(
        kernel,
        in_specs=[SSPEC] + [VSPEC] * 6,
        out_specs=[VSPEC] * len(outs),
        out_shape=outs,
        compiler_params=params(),
        name="adagrad",
    )(row_counts, row_lists, ids_column, head_grad, returned, table_t, state)


def swap_partner(values, mask, beside, *operands):
    count = lax.axis_size("dom")

    def branch(m):
        route = [(i, i ^ m) for i in range(count)]
        return lambda held, *rest: (lax.ppermute(held, "dom", route), beside(*rest))

    return lax.switch(mask - 1, [branch(m) for m in range(1, count)], values, *operands)


def body(
    embeddings,
    adagrad_state,
    relations,
    pairing,
    row_lists,
    row_counts,
    group_counts,
    head_ids,
    relation_ids,
    tail_slots,
    negatives,
):
    rounds = pairing.shape[0]
    rows = embeddings.shape[0]
    groups = head_ids.shape[1] // GROUP
    table_t = embeddings.T
    state = adagrad_state.reshape(1, rows)
    ids_column = row_lists.reshape(rounds, LIST, 1)

    def lanes(ids):
        ids = ids.reshape(rounds, groups, GROUP)
        ids = jnp.pad(ids, ((0, 0), (0, 0), (0, GPAD - GROUP)), constant_values=-1)
        return ids.reshape(rounds, groups, GPAD // 128, 128)

    tails = lanes(tail_slots)
    drawn = lanes(negatives)
    sent = first_sent(row_counts, row_lists, table_t)
    for r in range(rounds):
        if r == 0:
            incoming, scale = swap_partner(
                sent, pairing[r], gather_relations, relation_ids, relations.T
            )
        else:
            incoming, _ = swap_partner(sent, pairing[r], lambda: 0)
        block = lax.all_gather(incoming, "sub", axis=0, tiled=False)
        cat, flipped = make_queries(r, head_ids, table_t, scale, groups)
        share, block_grad = score_groups(r, group_counts, cat, flipped, block, tails, drawn)
        own_share, packed = reduce_block(share, block, block_grad)

        def heads(counts, ids, packed, scale):
            return head_gradients(r, counts, ids, packed, scale, rows)

        returned, head_grad = swap_partner(
            own_share, pairing[r], heads, group_counts, head_ids, packed, scale
        )
        last = r == rounds - 1
        done = adagrad(r, last, row_counts, row_lists, ids_column, head_grad, returned, table_t, state)
        table_t, state = done[0], done[1]
        if not last:
            sent = done[2]
    return (table_t.T, state.reshape(rows))


def solution(mesh):
    in_specs = (
        P(("dom", "sub"), None),
        P(("dom", "sub")),
        P(),
        P(),
        P(None, ("dom", "sub")),
        P(None, ("dom", "sub")),
        P(None, ("dom", "sub")),
        P(None, ("dom", "sub")),
        P(None, ("dom", "sub")),
        P(None, ("dom", "sub")),
        P(None, ("dom", "sub")),
    )
    out_specs = (P(("dom", "sub"), None), P(("dom", "sub")))
    return jax.shard_map(body, mesh=mesh, in_specs=in_specs, out_specs=out_specs, check_vma=False)
```

```python
import jax
import jax.numpy as jnp
from jax import lax
from jax.experimental import pallas as pl
from jax.experimental.pallas import tpu as pltpu
from jax.sharding import PartitionSpec as P

F32 = jnp.float32
BF16 = jnp.bfloat16
LOG2E = 1.4426950408889634
LEARN_RATE = 0.1

D = 400
FULL = 384
TAIL = D - FULL
GROUP = 1000
GPAD = 1024
LIST = 256
SUBS = 8
SLOTS = SUBS * LIST
STRIP = GPAD // 2
KCAT = 3 * FULL + 128
VMEM_LIMIT = 60 * 1024 * 1024

VSPEC = pl.BlockSpec(memory_space=pltpu.VMEM)
SSPEC = pl.BlockSpec(memory_space=pltpu.SMEM)
ANYSPEC = pl.BlockSpec(memory_space=pl.ANY)
UNROLL = 40


def split2(x):
    high = x.astype(BF16)
    return high, (x - high.astype(F32)).astype(BF16)


def split3(x):
    high, rest = split2(x)
    low = x - high.astype(F32) - rest.astype(F32)
    return high, rest, low.astype(BF16)


def dot(a, b):
    return lax.dot_general(a, b, (((1,), (0,)), ((), ())), preferred_element_type=F32)


def dot_nt(a, b):
    return lax.dot_general(a, b, (((1,), (1,)), ((), ())), preferred_element_type=F32)


def params(**more):
    return pltpu.CompilerParams(vmem_limit_bytes=VMEM_LIMIT, **more)


def cost(flops, moved):
    return pl.CostEstimate(flops=int(flops), bytes_accessed=int(moved), transcendentals=0)


def pack_rows(source, target, start, target_start):
    for j in range(4):
        if j < 3:
            tile = source[128 * j : 128 * (j + 1), pl.ds(start, 128)]
        else:
            tile = jnp.concatenate(
                [source[FULL:D, pl.ds(start, 128)], jnp.zeros((128 - TAIL, 128), F32)], axis=0
            )
        target[pl.ds(target_start + j, 128, stride=4), :] = tile.T


def relation_kernel(ids, table_hbm, out_hbm, table_t, packed, rows, load_sems, store_sems):
    tiles = table_hbm.shape[1] // 128
    pieces = load_sems.shape[0]
    bounds = [tiles * i // pieces * 128 for i in range(pieces + 1)]
    chunks = store_sems.shape[0]
    each = ids.shape[0] // chunks
    per_round = chunks // out_hbm.shape[0]

    def load(i):
        part = pl.ds(bounds[i], bounds[i + 1] - bounds[i])
        return pltpu.make_async_copy(table_hbm.at[:, part], table_t.at[:, part], load_sems.at[i])

    def store(c):
        return pltpu.make_async_copy(
            rows.at[pl.ds(c * each * 4, each * 4), :],
            out_hbm.at[c // per_round, pl.ds(c % per_round * each * 4, each * 4), :],
            store_sems.at[c],
        )

    for i in range(pieces):
        load(i).start()
    for i in range(pieces):
        load(i).wait()

        @pl.loop(bounds[i] // 128, bounds[i + 1] // 128)
        def _(tile):
            start = pl.multiple_of(tile * 128, 128)
            pack_rows(table_t, packed, start, start * 4)

    for c in range(chunks):

        @pl.loop(0, each // UNROLL)
        def _(i):
            first = c * each + i * UNROLL
            for u in range(UNROLL):
                row = pl.multiple_of(ids[first + u], 4)
                at = pl.multiple_of(first * 4 + 4 * u, 4)
                rows[pl.ds(at, 4), :] = packed[pl.ds(row, 4), :]

        store(c).start()
    for c in range(chunks):
        store(c).wait()


def gather_relations(starts, relations_t, rounds):
    count = relations_t.shape[1]
    edges = starts.shape[0] // rounds
    return pl.pallas_call(
        relation_kernel,
        in_specs=[SSPEC, ANYSPEC],
        out_specs=ANYSPEC,
        out_shape=jax.ShapeDtypeStruct((rounds, edges * 4, 128), F32),
        scratch_shapes=[
            pltpu.VMEM(relations_t.shape, F32),
            pltpu.VMEM((count * 4, 128), F32),
            pltpu.VMEM((rounds * edges * 4, 128), F32),
            pltpu.SemaphoreType.DMA((4,)),
            pltpu.SemaphoreType.DMA((rounds * edges // GROUP,)),
        ],
        compiler_params=params(),
        cost_estimate=cost(2e9, 60e6),
        name="relation_rows",
    )(starts, relations_t)


def pick_columns(table_t, ids_row, count):
    rows = table_t.shape[1]
    slot = lax.broadcasted_iota(jnp.int32, ids_row.shape, 1)
    wanted = jnp.where(slot < count, ids_row, -1)
    row = lax.broadcasted_iota(jnp.int32, (rows, LIST), 0)
    onehot = jnp.where(row == wanted, 1.0, 0.0).astype(BF16)
    high, mid, low = split3(table_t)
    return dot(high, onehot) + dot(mid, onehot) + dot(low, onehot)


def sent_kernel(counts, ids, table_t, out):
    out[...] = pick_columns(table_t[...], ids[0:1, :], counts[0, 0])


def first_sent(row_counts, row_lists, table_t):
    return pl.pallas_call(
        sent_kernel,
        in_specs=[SSPEC, VSPEC, VSPEC],
        out_specs=VSPEC,
        out_shape=jax.ShapeDtypeStruct((D, LIST), F32),
        compiler_params=params(),
        name="sent_rows",
    )(row_counts, row_lists, table_t)


def query_kernel(round_number, starts, table_t, scale, packed, table):
    g = pl.program_id(0)

    @pl.when(g == 0)
    def _():
        @pl.loop(0, table_t.shape[1] // 128)
        def _(i):
            start = pl.multiple_of(i * 128, 128)
            pack_rows(table_t, table, start, start * 4)

    base = (round_number * pl.num_programs(0) + g) * GROUP

    @pl.loop(0, GROUP // UNROLL)
    def _(i):
        for u in range(UNROLL):
            row = pl.ds(pl.multiple_of(starts[base + i * UNROLL + u], 4), 4)
            at = pl.ds(pl.multiple_of(i * (4 * UNROLL) + 4 * u, 4), 4)
            packed[at, :] = table[row, :] * scale[0, at, :]

    packed[4 * GROUP :, :] = jnp.zeros((4 * (GPAD - GROUP), 128), F32)


def make_queries(round_number, starts, table_t, scale):
    def kernel(*refs):
        query_kernel(round_number, *refs)

    groups = scale.shape[1] // (4 * GROUP)
    return pl.pallas_call(
        kernel,
        grid=(groups,),
        in_specs=[
            SSPEC,
            VSPEC,
            pl.BlockSpec((1, GROUP * 4, 128), lambda g: (round_number, g, 0)),
        ],
        out_specs=pl.BlockSpec((GPAD * 4, 128), lambda g: (g, 0)),
        out_shape=jax.ShapeDtypeStruct((groups * GPAD * 4, 128), F32),
        scratch_shapes=[pltpu.VMEM((table_t.shape[1] * 4, 128), F32)],
        compiler_params=params(),
        cost_estimate=cost(2e9, 20e6),
        name="queries",
    )(starts, table_t, scale)


def gather_kernel(
    own, packed_hbm, block, cat_hbm, flipped_hbm,
    packed, cat, flipped, own_sem, load_sems, cat_sems, flipped_sems,
    ring_send, ring_recv, mate_send, mate_recv,
):
    me = lax.axis_index("sub")
    x = me // 2
    core = me % 2
    chips = SUBS // 2
    mate = x * 2 + (1 - core)
    right = ((x + 1) % chips) * 2 + core
    left = ((x + chips - 1) % chips) * 2 + core
    across = ((x + 2) % chips) * 2 + core
    half = D // 2
    upper, lower = pl.ds(0, half), pl.ds(half, half)
    groups = cat.shape[0]
    rows_of = GPAD * 4

    def to(device, source, target, send, recv, n):
        return pltpu.make_async_remote_copy(
            src_ref=source,
            dst_ref=target,
            send_sem=send.at[n],
            recv_sem=recv.at[n],
            device_id={"sub": device},
            device_id_type=pl.DeviceIdType.MESH,
        )

    def load(g):
        return pltpu.make_async_copy(
            packed_hbm.at[pl.ds(g * rows_of, rows_of), :],
            packed.at[pl.ds(g * rows_of, rows_of), :],
            load_sems.at[g],
        )

    def store(g):
        return (
            pltpu.make_async_copy(cat.at[g], cat_hbm.at[g], cat_sems.at[g]),
            pltpu.make_async_copy(flipped.at[g], flipped_hbm.at[g], flipped_sems.at[g]),
        )

    for g in range(groups):
        load(g).start()
    keep = pltpu.make_async_copy(own, block.at[me], own_sem)
    keep.start()

    barrier = pltpu.get_barrier_semaphore()
    for other in (mate, right, left):
        pl.semaphore_signal(
            barrier, inc=1, device_id={"sub": other}, device_id_type=pl.DeviceIdType.MESH
        )
    pl.semaphore_wait(barrier, 3)

    ring = (
        to(right, own.at[upper], block.at[me, upper], ring_send, ring_recv, 0),
        to(left, own.at[lower], block.at[me, lower], ring_send, ring_recv, 1),
        to(right, own.at[lower], block.at[me, lower], ring_send, ring_recv, 2),
        to(left, own.at[upper], block.at[me, upper], ring_send, ring_recv, 3),
        to(right, block.at[left, upper], block.at[left, upper], ring_send, ring_recv, 4),
        to(left, block.at[right, lower], block.at[right, lower], ring_send, ring_recv, 5),
    )
    landed = (
        (left, upper),
        (right, lower),
        (left, lower),
        (right, upper),
        (across, upper),
        (across, lower),
    )
    own_to_mate = to(mate, own, block.at[me], mate_send, mate_recv, 6)
    to_mate = [
        to(mate, block.at[owner, part], block.at[owner, part], mate_send, mate_recv, n)
        for n, (owner, part) in enumerate(landed)
    ]

    for n in range(4):
        ring[n].start()
    own_to_mate.start()

    def operands(g):
        load(g).wait()

        @pl.loop(0, GPAD // 128)
        def _(b):
            rows = pl.ds(pl.multiple_of(b * 128, 128), 128)
            for j in range(4):
                tile = packed[pl.ds(g * rows_of + b * 512 + j, 128, stride=4), :]
                high, low = split2(tile * LOG2E)
                if j < 3:
                    cat[g, rows, 128 * j : 128 * (j + 1)] = high
                    cat[g, rows, FULL + 128 * j : FULL + 128 * (j + 1)] = high
                    cat[g, rows, 2 * FULL + 128 * j : 2 * FULL + 128 * (j + 1)] = low
                else:
                    high, low = high.astype(F32), low.astype(F32)
                    both = high + pltpu.roll(high, TAIL, 1) + pltpu.roll(low, 2 * TAIL, 1)
                    cat[g, rows, 3 * FULL :] = both.astype(BF16)
                high, low = split2(tile.T)
                width = 128 if j < 3 else TAIL
                flipped[g, 128 * j : 128 * j + width, rows] = high[:width]
                flipped[g, D + 128 * j : D + 128 * j + width, rows] = low[:width]

        for copy in store(g):
            copy.start()

    def pass_on(n):
        ring[n].wait_recv()
        if n < 2:
            ring[4 + n].start()
        to_mate[n].start()

    operands(0)
    pass_on(0)
    pass_on(1)
    operands(1)
    pass_on(2)
    pass_on(3)
    operands(2)
    pass_on(4)
    pass_on(5)
    for copy in ring:
        copy.wait_send()
    own_to_mate.wait()
    for copy in to_mate:
        copy.wait()
    keep.wait()
    for g in range(groups):
        for copy in store(g):
            copy.wait()


def gather_block(own, packed):
    groups = packed.shape[0] // (4 * GPAD)
    dma = pltpu.SemaphoreType.DMA
    shapes = [
        jax.ShapeDtypeStruct((SUBS, D, LIST), F32),
        jax.ShapeDtypeStruct((groups, GPAD, KCAT), BF16),
        jax.ShapeDtypeStruct((groups, 2 * D, GPAD), BF16),
    ]
    return pl.pallas_call(
        gather_kernel,
        in_specs=[ANYSPEC, ANYSPEC],
        out_specs=[ANYSPEC] * 3,
        out_shape=shapes,
        scratch_shapes=[
            pltpu.VMEM(packed.shape, F32),
            pltpu.VMEM(shapes[1].shape, BF16),
            pltpu.VMEM(shapes[2].shape, BF16),
            dma,
            dma((groups,)),
            dma((groups,)),
            dma((groups,)),
            dma((6,)),
            dma((6,)),
            dma((7,)),
            dma((7,)),
        ],
        compiler_params=params(collective_id=1, has_side_effects=True),
        cost_estimate=cost(2e9, 40e6),
        name="gather_block",
    )(own, packed)


def softmax_rows(first, group, active_rows, active, scores, share_high, share_low, tail_columns, bias):
    count = 16
    rows = pl.ds(first, count)
    tiles = SLOTS // 128
    lane = lax.broadcasted_iota(jnp.int32, (count, 128), 1).astype(F32)
    offset = tail_columns[active_rows, :] - lane
    own = None
    shifted = []
    top = None
    for j in range(tiles):
        raw = scores[rows, 128 * j : 128 * (j + 1)]
        hit = jnp.where(offset == 128.0 * j, raw, 0.0)
        own = hit if own is None else own + hit
        moved = raw + bias[group, j : j + 1, :]
        shifted.append(moved)
        top = moved if top is None else jnp.maximum(top, moved)
    positive = jnp.sum(own, axis=1, keepdims=True)
    top = jnp.maximum(jnp.max(top, axis=1, keepdims=True), positive)
    total = None
    weights = []
    for j in range(tiles):
        weight = jnp.exp2(shifted[j] - top)
        weights.append(weight)
        total = weight if total is None else total + weight
    negative_sum = jnp.sum(total, axis=1, keepdims=True)
    inverse = active / (jnp.exp2(positive - top) + negative_sum)
    own_share = -negative_sum * inverse
    for j in range(tiles):
        value = weights[j] * inverse + jnp.where(offset == 128.0 * j, own_share, 0.0)
        high, low = split2(value)
        share_high[rows, 128 * j : 128 * (j + 1)] = high
        share_low[rows, 128 * j : 128 * (j + 1)] = low


def score_kernel(
    round_number, counts, cat_hbm, flipped_hbm, block, tails, negatives, share_hbm, block_grad,
    cat, flipped, block_cat, scores_a, scores_b, high_a, high_b, low_a, low_b, tail_columns, bias,
    in_sems, out_sems,
):
    groups = cat.shape[0]
    strips = groups * 2
    scores = (scores_a, scores_b)
    highs = (high_a, high_b)
    lows = (low_a, low_b)

    def load(g):
        return (
            pltpu.make_async_copy(cat_hbm.at[g], cat.at[g], in_sems.at[g, 0]),
            pltpu.make_async_copy(flipped_hbm.at[g], flipped.at[g], in_sems.at[g, 1]),
        )

    def store(t):
        target = pl.ds((t % 2) * STRIP, STRIP)
        return (
            pltpu.make_async_copy(highs[t % 2], share_hbm.at[t // 2, 0, target, :], out_sems.at[t % 2, 0]),
            pltpu.make_async_copy(lows[t % 2], share_hbm.at[t // 2, 1, target, :], out_sems.at[t % 2, 1]),
        )

    for g in range(groups):
        for copy in load(g):
            copy.start()

    @pl.loop(0, SUBS)
    def _(s):
        high, low = split2(block[s])
        block_cat[s, 0:FULL, :] = high[:FULL]
        block_cat[s, FULL : 2 * FULL, :] = low[:FULL]
        block_cat[s, 2 * FULL : 3 * FULL, :] = high[:FULL]
        block_cat[s, 3 * FULL : 3 * FULL + TAIL, :] = high[FULL:]
        block_cat[s, 3 * FULL + TAIL : 3 * FULL + 2 * TAIL, :] = low[FULL:]
        block_cat[s, 3 * FULL + 2 * TAIL : 3 * FULL + 3 * TAIL, :] = high[FULL:]
        block_cat[s, 3 * FULL + 3 * TAIL :, :] = jnp.zeros((128 - 3 * TAIL, LIST), BF16)
        block_grad[s] = jnp.zeros((D, LIST), F32)

    low_iota = lax.broadcasted_iota(jnp.int32, (128, 128), 0)
    high_iota = lax.broadcasted_iota(jnp.int32, (16, 128), 0)
    for g in range(groups):
        drawn = negatives[round_number, g]
        total = jnp.zeros((16, 128), F32)
        tail = tails[round_number, g].astype(F32)
        for b in range(GPAD // 128):
            row = drawn[b : b + 1, :]
            low_hot = jnp.where(low_iota == jnp.bitwise_and(row, 127), 1.0, 0.0).astype(BF16)
            high_hot = jnp.where(high_iota == jnp.right_shift(row, 7), 1.0, 0.0).astype(BF16)
            total = total + dot_nt(high_hot, low_hot)
            first = g * GPAD + 128 * b
            tail_columns[first : first + 128, :] = jnp.broadcast_to(tail[b : b + 1, :], (128, 128)).T
        bias[g] = jnp.where(total > 0.5, jnp.log2(jnp.maximum(total, 1.0)), -1e30)

    for stage in range(strips + 2):
        if stage < strips and stage % 2 == 0:
            for copy in load(stage // 2):
                copy.wait()
        if stage >= 3 and stage - 3 < strips - 2:
            for copy in store(stage - 3):
                copy.wait()

        @pl.loop(0, SUBS)
        def _(s):
            at = pl.ds(pl.multiple_of(s * LIST, LIST), LIST)
            if stage < strips:
                t = stage
                edges = slice((t % 2) * STRIP, (t % 2 + 1) * STRIP)
                scores[t % 2][:, at] = dot(cat[t // 2, edges, :], block_cat[s])
            if 2 <= stage:
                t = stage - 2
                edges = slice((t % 2) * STRIP, (t % 2 + 1) * STRIP)
                high = highs[t % 2][:, at]
                both = dot(flipped[t // 2, :, edges], high)
                cross = dot(flipped[t // 2, :D, edges], lows[t % 2][:, at])
                block_grad[s] += both[:D] + both[D:] + cross
            if 1 <= stage <= strips:
                t = stage - 1
                g = t // 2
                part = STRIP // SUBS
                row_iota = lax.broadcasted_iota(jnp.int32, (16, 1), 0)
                used = jnp.where(g < counts[round_number, 0], GROUP, 0)
                for u in range(part // 16):
                    first = pl.multiple_of(s * part + u * 16, 16)
                    in_group = first + (t % 2) * STRIP
                    softmax_rows(
                        first,
                        g,
                        pl.ds(pl.multiple_of(in_group + g * GPAD, 16), 16),
                        jnp.where(row_iota + in_group < used, 1.0, 0.0),
                        scores[t % 2],
                        highs[t % 2],
                        lows[t % 2],
                        tail_columns,
                        bias,
                    )

        if 1 <= stage <= strips:
            for copy in store(stage - 1):
                copy.start()

    for t in (strips - 2, strips - 1):
        for copy in store(t):
            copy.wait()


def score_groups(round_number, group_counts, cat, flipped, block, tails, negatives):
    def kernel(*refs):
        score_kernel(round_number, *refs)

    groups = cat.shape[0]
    anywhere = pl.BlockSpec(memory_space=pl.ANY)
    return pl.pallas_call(
        kernel,
        in_specs=[SSPEC, anywhere, anywhere, VSPEC, VSPEC, VSPEC],
        out_specs=[anywhere, VSPEC],
        out_shape=[
            jax.ShapeDtypeStruct((groups, 2, GPAD, SLOTS), BF16),
            jax.ShapeDtypeStruct((SUBS, D, LIST), F32),
        ],
        scratch_shapes=[
            pltpu.VMEM(cat.shape, BF16),
            pltpu.VMEM(flipped.shape, BF16),
            pltpu.VMEM((SUBS, KCAT, LIST), BF16),
            pltpu.VMEM((STRIP, SLOTS), F32),
            pltpu.VMEM((STRIP, SLOTS), F32),
            pltpu.VMEM((STRIP, SLOTS), BF16),
            pltpu.VMEM((STRIP, SLOTS), BF16),
            pltpu.VMEM((STRIP, SLOTS), BF16),
            pltpu.VMEM((STRIP, SLOTS), BF16),
            pltpu.VMEM((groups * GPAD, 128), F32),
            pltpu.VMEM((groups, 16, 128), F32),
            pltpu.SemaphoreType.DMA((groups, 2)),
            pltpu.SemaphoreType.DMA((2, 2)),
        ],
        compiler_params=params(),
        cost_estimate=cost(40e9, 60e6),
        name="scores",
    )(group_counts, cat, flipped, block, tails, negatives)


def reduce_kernel(
    share_hbm, block, block_grad, own_share, packed,
    rows_high, rows_low, parts, from_mate, sums, relay_ahead, relay_behind, from_left, from_right,
    load_sems, mate_send, mate_recv, ring_send, ring_recv,
):
    me = lax.axis_index("sub")
    x = me // 2
    core = me % 2
    chips = SUBS // 2
    mate = x * 2 + (1 - core)
    right = ((x + 1) % chips) * 2 + core
    left = ((x + chips - 1) % chips) * 2 + core
    half = D // 2
    upper, lower = pl.ds(0, half), pl.ds(half, half)
    groups = share_hbm.shape[0]
    strips = groups * 2

    def block_of(k, c):
        return ((x + k) % chips) * 2 + c

    def load(t):
        slot = t % 2
        return pltpu.make_async_copy(
            share_hbm.at[t // 2, :, pl.ds(pl.multiple_of(slot * STRIP, STRIP), STRIP), :],
            parts.at[slot],
            load_sems.at[slot],
        )

    def to(device, source, target, send, recv, n):
        return pltpu.make_async_remote_copy(
            src_ref=source,
            dst_ref=target,
            send_sem=send.at[n],
            recv_sem=recv.at[n],
            device_id={"sub": device},
            device_id_type=pl.DeviceIdType.MESH,
        )

    load(0).start()
    barrier = pltpu.get_barrier_semaphore()
    for other in (mate, right, left):
        pl.semaphore_signal(
            barrier, inc=1, device_id={"sub": other}, device_id_type=pl.DeviceIdType.MESH
        )
    pl.semaphore_wait(barrier, 3)

    mates = {
        k: to(mate, block_grad.at[block_of(k, 1 - core)], from_mate.at[k], mate_send, mate_recv, k)
        for k in range(chips)
    }
    for k in (2, 1, 3, 0):
        mates[k].start()
    ring = (
        to(right, sums.at[2, upper], relay_ahead, ring_send, ring_recv, 0),
        to(left, sums.at[2, lower], relay_behind, ring_send, ring_recv, 1),
        to(right, sums.at[1, lower], from_left.at[lower], ring_send, ring_recv, 2),
        to(left, sums.at[3, upper], from_right.at[upper], ring_send, ring_recv, 3),
        to(right, sums.at[1, upper], from_left.at[upper], ring_send, ring_recv, 4),
        to(left, sums.at[3, lower], from_right.at[lower], ring_send, ring_recv, 5),
    )

    @pl.loop(0, SUBS)
    def _(s):
        for h in range(LIST // 128):
            rows = pl.ds(pl.multiple_of(s * LIST + h * 128, 128), 128)
            for j in range(4):
                lanes = slice(128 * h, 128 * (h + 1))
                if j < 3:
                    tile = block[s, 128 * j : 128 * (j + 1), lanes]
                else:
                    tile = jnp.concatenate(
                        [block[s, FULL:D, lanes], jnp.zeros((128 - TAIL, 128), F32)], axis=0
                    )
                high, low = split2(tile.T)
                rows_high[rows, 128 * j : 128 * (j + 1)] = high
                rows_low[rows, 128 * j : 128 * (j + 1)] = low

    def query_strip(t, more):
        if more:
            load(t + 1).start()
        load(t).wait()
        slot = t % 2
        for n in range(2):
            at = slice(256 * n, 256 * (n + 1))
            grad = (
                dot(parts[slot, 0], rows_high[:, at])
                + dot(parts[slot, 0], rows_low[:, at])
                + dot(parts[slot, 1], rows_high[:, at])
            )
            for h in range(2):
                for b in range(STRIP // 128):
                    packed[pl.ds(t * (4 * STRIP) + 512 * b + 2 * n + h, 128, stride=4), :] = grad[
                        128 * b : 128 * (b + 1), 128 * h : 128 * (h + 1)
                    ]

    def pair_sum(k):
        mates[k].wait()
        sums[k] = block_grad[block_of(k, core)] + from_mate[k]

    pair_sum(2)
    ring[0].start()
    ring[1].start()
    pair_sum(1)
    ring[2].start()
    pair_sum(3)
    ring[3].start()
    pair_sum(0)

    @pl.loop(0, 2)
    def _(t):
        query_strip(t, True)

    ring[0].wait()
    sums[1, upper, :] += relay_ahead[...]
    ring[4].start()
    ring[1].wait()
    sums[3, lower, :] += relay_behind[...]
    ring[5].start()

    @pl.loop(2, strips - 1)
    def _(t):
        query_strip(t, True)

    query_strip(strips - 1, False)

    for n in (2, 3, 4, 5):
        ring[n].wait()
    own_share[...] = sums[0] + from_left[...] + from_right[...]


def reduce_block(share, block, block_grad):
    groups = share.shape[0]
    return pl.pallas_call(
        reduce_kernel,
        in_specs=[pl.BlockSpec(memory_space=pl.ANY), VSPEC, VSPEC],
        out_specs=[VSPEC, VSPEC],
        out_shape=[
            jax.ShapeDtypeStruct((D, LIST), F32),
            jax.ShapeDtypeStruct((groups * GPAD * 4, 128), F32),
        ],
        scratch_shapes=[
            pltpu.VMEM((SLOTS, 512), BF16),
            pltpu.VMEM((SLOTS, 512), BF16),
            pltpu.VMEM((2, 2, STRIP, SLOTS), BF16),
            pltpu.VMEM((SUBS // 2, D, LIST), F32),
            pltpu.VMEM((SUBS // 2, D, LIST), F32),
            pltpu.VMEM((D // 2, LIST), F32),
            pltpu.VMEM((D // 2, LIST), F32),
            pltpu.VMEM((D, LIST), F32),
            pltpu.VMEM((D, LIST), F32),
            pltpu.SemaphoreType.DMA((2,)),
            pltpu.SemaphoreType.DMA((4,)),
            pltpu.SemaphoreType.DMA((4,)),
            pltpu.SemaphoreType.DMA((6,)),
            pltpu.SemaphoreType.DMA((6,)),
        ],
        compiler_params=params(collective_id=0, has_side_effects=True),
        cost_estimate=cost(20e9, 60e6),
        name="reduce_block",
    )(share, block, block_grad)


def head_kernel(round_number, counts, starts, packed, scale, out, *sums):
    g = pl.program_id(0)
    parts = len(sums)

    @pl.when(g == 0)
    def _():
        for part in sums:
            part[...] = jnp.zeros_like(part)

    @pl.when(g < counts[round_number, 0])
    def _():
        base = (round_number * pl.num_programs(0) + g) * GROUP

        @pl.loop(0, GROUP // parts, unroll=5)
        def _(i):
            news = []
            for u in range(parts):
                e = i * parts + u
                row = pl.ds(pl.multiple_of(starts[base + e], 4), 4)
                at = pl.ds(pl.multiple_of(e * 4, 4), 4)
                term = packed[at, :] * scale[0, at, :]
                news.append((row, sums[u][row, :] + term))
            for u in range(parts):
                row, value = news[u]
                sums[u][row, :] = value

    @pl.when(g == pl.num_programs(0) - 1)
    def _():
        @pl.loop(0, out.shape[1] // 128)
        def _(i):
            columns = pl.ds(pl.multiple_of(i * 128, 128), 128)
            for j in range(4):
                at = pl.ds(i * 512 + j, 128, stride=4)
                tile = sums[0][at, :]
                for part in sums[1:]:
                    tile = tile + part[at, :]
                width = 128 if j < 3 else TAIL
                out[128 * j : 128 * j + width, columns] = tile.T[:width]


def head_gradients(round_number, group_counts, starts, packed, scale, rows):
    def kernel(*refs):
        head_kernel(round_number, *refs)

    groups = packed.shape[0] // (GPAD * 4)
    parts = 4
    return pl.pallas_call(
        kernel,
        grid=(groups,),
        in_specs=[
            SSPEC,
            SSPEC,
            pl.BlockSpec((GPAD * 4, 128), lambda g: (g, 0)),
            pl.BlockSpec((1, GROUP * 4, 128), lambda g: (round_number, g, 0)),
        ],
        out_specs=VSPEC,
        out_shape=jax.ShapeDtypeStruct((D, rows), F32),
        scratch_shapes=[pltpu.VMEM((rows * 4, 128), F32)] * parts,
        compiler_params=params(),
        cost_estimate=cost(2e9, 40e6),
        name="head_gradients",
    )(group_counts, starts, packed, scale)


def adagrad_kernel(
    round_number, last, counts, ids, ids_column, head_grad, returned, table_t, state,
    new_table_t, new_state, *sent,
):
    rows = table_t.shape[1]
    width = 512
    wanted = ids_column[round_number]
    slot = lax.broadcasted_iota(jnp.int32, wanted.shape, 0)
    wanted = jnp.where(slot < counts[round_number, 0], wanted, -1)
    high, mid, low = split3(returned[...])
    for first in range(0, rows, width):
        at = slice(first, first + width)
        row = lax.broadcasted_iota(jnp.int32, (LIST, width), 1) + first
        onehot = jnp.where(row == wanted, 1.0, 0.0).astype(BF16)
        totals = head_grad[:, at] + (dot(high, onehot) + dot(mid, onehot) + dot(low, onehot))
        fresh = state[:, at] + jnp.sum(totals * totals, axis=0, keepdims=True) / D
        new_state[:, at] = fresh
        new_table_t[:, at] = table_t[:, at] - LEARN_RATE * totals / jnp.sqrt(fresh)
    if not last:
        sent[0][...] = pick_columns(
            new_table_t[...], ids[round_number + 1 : round_number + 2, :], counts[round_number + 1, 0]
        )


def adagrad(round_number, last, row_counts, row_lists, ids_column, head_grad, returned, table_t, state):
    def kernel(*refs):
        adagrad_kernel(round_number, last, *refs)

    outs = [jax.ShapeDtypeStruct(table_t.shape, F32), jax.ShapeDtypeStruct(state.shape, F32)]
    if not last:
        outs.append(jax.ShapeDtypeStruct((D, LIST), F32))
    return pl.pallas_call(
        kernel,
        in_specs=[SSPEC] + [VSPEC] * 6,
        out_specs=[VSPEC] * len(outs),
        out_shape=outs,
        compiler_params=params(),
        name="adagrad",
    )(row_counts, row_lists, ids_column, head_grad, returned, table_t, state)


def swap_partner(values, mask, beside, *operands):
    count = lax.axis_size("dom")

    def branch(m):
        route = [(i, i ^ m) for i in range(count)]
        return lambda held, *rest: (lax.ppermute(held, "dom", route), beside(*rest))

    return lax.switch(mask - 1, [branch(m) for m in range(1, count)], values, *operands)


def body(
    embeddings,
    adagrad_state,
    relations,
    pairing,
    row_lists,
    row_counts,
    group_counts,
    head_ids,
    relation_ids,
    tail_slots,
    negatives,
):
    rounds = pairing.shape[0]
    rows = embeddings.shape[0]
    groups = head_ids.shape[1] // GROUP
    table_t = embeddings.T
    state = adagrad_state.reshape(1, rows)
    ids_column = row_lists.reshape(rounds, LIST, 1)

    def lanes(ids):
        ids = ids.reshape(rounds, groups, GROUP)
        ids = jnp.pad(ids, ((0, 0), (0, 0), (0, GPAD - GROUP)), constant_values=-1)
        return ids.reshape(rounds, groups, GPAD // 128, 128)

    tails = lanes(tail_slots)
    drawn = lanes(negatives)
    sent = first_sent(row_counts, row_lists, table_t)
    head_starts = head_ids.reshape(-1) * 4
    relation_starts = relation_ids.reshape(-1) * 4

    def first_queries(relation_starts, relations_t, head_starts, table_t):
        scale = gather_relations(relation_starts, relations_t, rounds)
        return scale, make_queries(0, head_starts, table_t, scale)

    for r in range(rounds):
        if r == 0:
            incoming, (scale, packed) = swap_partner(
                sent, pairing[r], first_queries, relation_starts, relations.T, head_starts, table_t
            )
        else:

            def later_queries(head_starts, table_t, scale):
                return make_queries(r, head_starts, table_t, scale)

            incoming, packed = swap_partner(
                sent, pairing[r], later_queries, head_starts, table_t, scale
            )
        block, cat, flipped = gather_block(incoming, packed)
        share, block_grad = score_groups(r, group_counts, cat, flipped, block, tails, drawn)
        own_share, packed = reduce_block(share, block, block_grad)

        def heads(counts, starts, packed, scale):
            return head_gradients(r, counts, starts, packed, scale, rows)

        returned, head_grad = swap_partner(
            own_share, pairing[r], heads, group_counts, head_starts, packed, scale
        )
        last = r == rounds - 1
        done = adagrad(r, last, row_counts, row_lists, ids_column, head_grad, returned, table_t, state)
        table_t, state = done[0], done[1]
        if not last:
            sent = done[2]
    return (table_t.T, state.reshape(rows))


def solution(mesh):
    in_specs = (
        P(("dom", "sub"), None),
        P(("dom", "sub")),
        P(),
        P(),
        P(None, ("dom", "sub")),
        P(None, ("dom", "sub")),
        P(None, ("dom", "sub")),
        P(None, ("dom", "sub")),
        P(None, ("dom", "sub")),
        P(None, ("dom", "sub")),
        P(None, ("dom", "sub")),
    )
    out_specs = (P(("dom", "sub"), None), P(("dom", "sub")))
    return jax.shard_map(body, mesh=mesh, in_specs=in_specs, out_specs=out_specs, check_vma=False)
```

```python
import jax
import jax.numpy as jnp
from jax import lax
from jax.experimental import pallas as pl
from jax.experimental.pallas import tpu as pltpu
from jax.sharding import PartitionSpec as P

F32 = jnp.float32
BF16 = jnp.bfloat16
LOG2E = 1.4426950408889634
LEARN_RATE = 0.1

D = 400
FULL = 384
TAIL = D - FULL
GROUP = 1000
GPAD = 1024
LIST = 256
SUBS = 8
SLOTS = SUBS * LIST
STRIP = GPAD // 2
KCAT = 3 * FULL + 128
VMEM_LIMIT = 60 * 1024 * 1024

VSPEC = pl.BlockSpec(memory_space=pltpu.VMEM)
SSPEC = pl.BlockSpec(memory_space=pltpu.SMEM)
ANYSPEC = pl.BlockSpec(memory_space=pl.ANY)
UNROLL = 20


def split2(x):
    high = x.astype(BF16)
    return high, (x - high.astype(F32)).astype(BF16)


def split3(x):
    high, rest = split2(x)
    low = x - high.astype(F32) - rest.astype(F32)
    return high, rest, low.astype(BF16)


def dot(a, b):
    return lax.dot_general(a, b, (((1,), (0,)), ((), ())), preferred_element_type=F32)


def dot_nt(a, b):
    return lax.dot_general(a, b, (((1,), (1,)), ((), ())), preferred_element_type=F32)


def params(**more):
    return pltpu.CompilerParams(vmem_limit_bytes=VMEM_LIMIT, **more)


def cost(flops, moved):
    return pl.CostEstimate(flops=int(flops), bytes_accessed=int(moved), transcendentals=0)


def pack_rows(source, target, start, target_start):
    for j in range(4):
        if j < 3:
            tile = source[128 * j : 128 * (j + 1), pl.ds(start, 128)]
        else:
            tile = jnp.concatenate(
                [source[FULL:D, pl.ds(start, 128)], jnp.zeros((128 - TAIL, 128), F32)], axis=0
            )
        target[pl.ds(target_start + j, 128, stride=4), :] = tile.T


def relation_kernel(ids, table_hbm, out_hbm, table_t, packed, rows, load_sems, store_sems):
    pieces = load_sems.shape[0]
    width = table_hbm.shape[1] // pieces
    chunks = store_sems.shape[0]
    each = ids.shape[0] // chunks
    per_round = chunks // out_hbm.shape[0]

    def load(i):
        part = pl.ds(pl.multiple_of(i * width, 128), width)
        return pltpu.make_async_copy(table_hbm.at[:, part], table_t.at[:, part], load_sems.at[i])

    def store(c):
        return pltpu.make_async_copy(
            rows.at[pl.ds(pl.multiple_of(c * each * 4, 8), each * 4), :],
            out_hbm.at[c // per_round, pl.ds(pl.multiple_of(c % per_round * each * 4, 8), each * 4), :],
            store_sems.at[c],
        )

    for i in range(pieces):
        load(i).start()

    @pl.loop(0, pieces)
    def _(i):
        load(i).wait()

        @pl.loop(0, width // 128)
        def _(tile):
            start = pl.multiple_of(i * width + tile * 128, 128)
            pack_rows(table_t, packed, start, start * 4)

    @pl.loop(0, chunks)
    def _(c):
        @pl.loop(0, each // UNROLL)
        def _(i):
            first = c * each + i * UNROLL
            for u in range(UNROLL):
                row = pl.multiple_of(ids[first + u], 4)
                at = pl.multiple_of(first * 4 + 4 * u, 4)
                rows[pl.ds(at, 4), :] = packed[pl.ds(row, 4), :]

        store(c).start()

    for c in range(chunks):
        store(c).wait()


def gather_relations(starts, relations_t, rounds):
    count = relations_t.shape[1]
    edges = starts.shape[0] // rounds
    return pl.pallas_call(
        relation_kernel,
        in_specs=[SSPEC, ANYSPEC],
        out_specs=ANYSPEC,
        out_shape=jax.ShapeDtypeStruct((rounds, edges * 4, 128), F32),
        scratch_shapes=[
            pltpu.VMEM(relations_t.shape, F32),
            pltpu.VMEM((count * 4, 128), F32),
            pltpu.VMEM((rounds * edges * 4, 128), F32),
            pltpu.SemaphoreType.DMA((2,)),
            pltpu.SemaphoreType.DMA((rounds * edges // GROUP,)),
        ],
        compiler_params=params(),
        cost_estimate=cost(2e9, 60e6),
        name="relation_rows",
    )(starts, relations_t)


def pick_columns(table_t, ids_row, count):
    rows = table_t.shape[1]
    slot = lax.broadcasted_iota(jnp.int32, ids_row.shape, 1)
    wanted = jnp.where(slot < count, ids_row, -1)
    row = lax.broadcasted_iota(jnp.int32, (rows, LIST), 0)
    onehot = jnp.where(row == wanted, 1.0, 0.0).astype(BF16)
    high, mid, low = split3(table_t)
    return dot(high, onehot) + dot(mid, onehot) + dot(low, onehot)


def sent_kernel(counts, ids, table_t, out):
    out[...] = pick_columns(table_t[...], ids[0:1, :], counts[0, 0])


def first_sent(row_counts, row_lists, table_t):
    return pl.pallas_call(
        sent_kernel,
        in_specs=[SSPEC, VSPEC, VSPEC],
        out_specs=VSPEC,
        out_shape=jax.ShapeDtypeStruct((D, LIST), F32),
        compiler_params=params(),
        name="sent_rows",
    )(row_counts, row_lists, table_t)


def query_kernel(round_number, starts, table_t, scale, packed, table):
    g = pl.program_id(0)

    @pl.when(g == 0)
    def _():
        @pl.loop(0, table_t.shape[1] // 128)
        def _(i):
            start = pl.multiple_of(i * 128, 128)
            pack_rows(table_t, table, start, start * 4)

    base = (round_number * pl.num_programs(0) + g) * GROUP

    @pl.loop(0, GROUP // UNROLL)
    def _(i):
        for u in range(UNROLL):
            row = pl.ds(pl.multiple_of(starts[base + i * UNROLL + u], 4), 4)
            at = pl.ds(pl.multiple_of(i * (4 * UNROLL) + 4 * u, 4), 4)
            packed[at, :] = table[row, :] * scale[0, at, :]

    packed[4 * GROUP :, :] = jnp.zeros((4 * (GPAD - GROUP), 128), F32)


def make_queries(round_number, starts, table_t, scale):
    def kernel(*refs):
        query_kernel(round_number, *refs)

    groups = scale.shape[1] // (4 * GROUP)
    return pl.pallas_call(
        kernel,
        grid=(groups,),
        in_specs=[
            SSPEC,
            VSPEC,
            pl.BlockSpec((1, GROUP * 4, 128), lambda g: (round_number, g, 0)),
        ],
        out_specs=pl.BlockSpec((GPAD * 4, 128), lambda g: (g, 0)),
        out_shape=jax.ShapeDtypeStruct((groups * GPAD * 4, 128), F32),
        scratch_shapes=[pltpu.VMEM((table_t.shape[1] * 4, 128), F32)],
        compiler_params=params(),
        cost_estimate=cost(2e9, 20e6),
        name="queries",
    )(starts, table_t, scale)


def gather_kernel(
    own, packed_hbm, block, cat_hbm, flipped_hbm,
    packed, cat, flipped, own_sem, load_sems, cat_sems, flipped_sems,
    ring_send, ring_recv, mate_send, mate_recv,
):
    me = lax.axis_index("sub")
    x = me // 2
    core = me % 2
    chips = SUBS // 2
    mate = x * 2 + (1 - core)
    right = ((x + 1) % chips) * 2 + core
    left = ((x + chips - 1) % chips) * 2 + core
    across = ((x + 2) % chips) * 2 + core
    half = D // 2
    upper, lower = pl.ds(0, half), pl.ds(half, half)
    groups = cat.shape[0]
    rows_of = GPAD * 4

    def to(device, source, target, send, recv, n):
        return pltpu.make_async_remote_copy(
            src_ref=source,
            dst_ref=target,
            send_sem=send.at[n],
            recv_sem=recv.at[n],
            device_id={"sub": device},
            device_id_type=pl.DeviceIdType.MESH,
        )

    def load(g):
        return pltpu.make_async_copy(
            packed_hbm.at[pl.ds(g * rows_of, rows_of), :],
            packed.at[pl.ds(g * rows_of, rows_of), :],
            load_sems.at[g],
        )

    def store(g):
        return (
            pltpu.make_async_copy(cat.at[g], cat_hbm.at[g], cat_sems.at[g]),
            pltpu.make_async_copy(flipped.at[g], flipped_hbm.at[g], flipped_sems.at[g]),
        )

    for g in range(groups):
        load(g).start()
    keep = pltpu.make_async_copy(own, block.at[me], own_sem)
    keep.start()

    barrier = pltpu.get_barrier_semaphore()
    for other in (mate, right, left):
        pl.semaphore_signal(
            barrier, inc=1, device_id={"sub": other}, device_id_type=pl.DeviceIdType.MESH
        )
    pl.semaphore_wait(barrier, 3)

    ring = (
        to(right, own.at[upper], block.at[me, upper], ring_send, ring_recv, 0),
        to(left, own.at[lower], block.at[me, lower], ring_send, ring_recv, 1),
        to(right, own.at[lower], block.at[me, lower], ring_send, ring_recv, 2),
        to(left, own.at[upper], block.at[me, upper], ring_send, ring_recv, 3),
        to(right, block.at[left, upper], block.at[left, upper], ring_send, ring_recv, 4),
        to(left, block.at[right, lower], block.at[right, lower], ring_send, ring_recv, 5),
    )
    landed = (
        (left, upper),
        (right, lower),
        (left, lower),
        (right, upper),
        (across, upper),
        (across, lower),
    )
    own_to_mate = to(mate, own, block.at[me], mate_send, mate_recv, 6)
    to_mate = [
        to(mate, block.at[owner, part], block.at[owner, part], mate_send, mate_recv, n)
        for n, (owner, part) in enumerate(landed)
    ]

    for n in range(4):
        ring[n].start()
    own_to_mate.start()

    def operands(g):
        load(g).wait()

        @pl.loop(0, GPAD // 128)
        def _(b):
            rows = pl.ds(pl.multiple_of(b * 128, 128), 128)
            for j in range(4):
                tile = packed[pl.ds(g * rows_of + b * 512 + j, 128, stride=4), :]
                high, low = split2(tile * LOG2E)
                if j < 3:
                    cat[g, rows, 128 * j : 128 * (j + 1)] = high
                    cat[g, rows, FULL + 128 * j : FULL + 128 * (j + 1)] = high
                    cat[g, rows, 2 * FULL + 128 * j : 2 * FULL + 128 * (j + 1)] = low
                else:
                    high, low = high.astype(F32), low.astype(F32)
                    both = high + pltpu.roll(high, TAIL, 1) + pltpu.roll(low, 2 * TAIL, 1)
                    cat[g, rows, 3 * FULL :] = both.astype(BF16)
                high, low = split2(tile.T)
                width = 128 if j < 3 else TAIL
                flipped[g, 128 * j : 128 * j + width, rows] = high[:width]
                flipped[g, D + 128 * j : D + 128 * j + width, rows] = low[:width]

        for copy in store(g):
            copy.start()

    def pass_on(n):
        ring[n].wait_recv()
        if n < 2:
            ring[4 + n].start()
        to_mate[n].start()

    operands(0)
    pass_on(0)
    pass_on(1)
    operands(1)
    pass_on(2)
    pass_on(3)
    operands(2)
    pass_on(4)
    pass_on(5)
    for copy in ring:
        copy.wait_send()
    own_to_mate.wait()
    for copy in to_mate:
        copy.wait()
    keep.wait()
    for g in range(groups):
        for copy in store(g):
            copy.wait()


def gather_block(own, packed):
    groups = packed.shape[0] // (4 * GPAD)
    dma = pltpu.SemaphoreType.DMA
    shapes = [
        jax.ShapeDtypeStruct((SUBS, D, LIST), F32),
        jax.ShapeDtypeStruct((groups, GPAD, KCAT), BF16),
        jax.ShapeDtypeStruct((groups, 2 * D, GPAD), BF16),
    ]
    return pl.pallas_call(
        gather_kernel,
        in_specs=[ANYSPEC, ANYSPEC],
        out_specs=[ANYSPEC] * 3,
        out_shape=shapes,
        scratch_shapes=[
            pltpu.VMEM(packed.shape, F32),
            pltpu.VMEM(shapes[1].shape, BF16),
            pltpu.VMEM(shapes[2].shape, BF16),
            dma,
            dma((groups,)),
            dma((groups,)),
            dma((groups,)),
            dma((6,)),
            dma((6,)),
            dma((7,)),
            dma((7,)),
        ],
        compiler_params=params(collective_id=1, has_side_effects=True),
        cost_estimate=cost(2e9, 40e6),
        name="gather_block",
    )(own, packed)


def softmax_rows(first, group, active_rows, active, scores, share_high, share_low, tail_columns, bias):
    count = 16
    rows = pl.ds(first, count)
    tiles = SLOTS // 128
    lane = lax.broadcasted_iota(jnp.int32, (count, 128), 1).astype(F32)
    offset = tail_columns[active_rows, :] - lane
    own = None
    shifted = []
    top = None
    for j in range(tiles):
        raw = scores[rows, 128 * j : 128 * (j + 1)]
        hit = jnp.where(offset == 128.0 * j, raw, 0.0)
        own = hit if own is None else own + hit
        moved = raw + bias[group, j : j + 1, :]
        shifted.append(moved)
        top = moved if top is None else jnp.maximum(top, moved)
    positive = jnp.sum(own, axis=1, keepdims=True)
    top = jnp.maximum(jnp.max(top, axis=1, keepdims=True), positive)
    total = None
    weights = []
    for j in range(tiles):
        weight = jnp.exp2(shifted[j] - top)
        weights.append(weight)
        total = weight if total is None else total + weight
    negative_sum = jnp.sum(total, axis=1, keepdims=True)
    inverse = active / (jnp.exp2(positive - top) + negative_sum)
    own_share = -negative_sum * inverse
    for j in range(tiles):
        value = weights[j] * inverse + jnp.where(offset == 128.0 * j, own_share, 0.0)
        high, low = split2(value)
        share_high[rows, 128 * j : 128 * (j + 1)] = high
        share_low[rows, 128 * j : 128 * (j + 1)] = low


def score_kernel(
    round_number, counts, cat_hbm, flipped_hbm, block, tails, negatives, share_hbm, block_grad,
    cat, flipped, block_cat, scores_a, scores_b, high_a, high_b, low_a, low_b, tail_columns, bias,
    in_sems, out_sems,
):
    groups = cat.shape[0]
    strips = groups * 2
    scores = (scores_a, scores_b)
    highs = (high_a, high_b)
    lows = (low_a, low_b)

    def load(g):
        return (
            pltpu.make_async_copy(cat_hbm.at[g], cat.at[g], in_sems.at[g, 0]),
            pltpu.make_async_copy(flipped_hbm.at[g], flipped.at[g], in_sems.at[g, 1]),
        )

    def store(t):
        target = pl.ds((t % 2) * STRIP, STRIP)
        return (
            pltpu.make_async_copy(highs[t % 2], share_hbm.at[t // 2, 0, target, :], out_sems.at[t % 2, 0]),
            pltpu.make_async_copy(lows[t % 2], share_hbm.at[t // 2, 1, target, :], out_sems.at[t % 2, 1]),
        )

    for g in range(groups):
        for copy in load(g):
            copy.start()

    @pl.loop(0, SUBS)
    def _(s):
        high, low = split2(block[s])
        block_cat[s, 0:FULL, :] = high[:FULL]
        block_cat[s, FULL : 2 * FULL, :] = low[:FULL]
        block_cat[s, 2 * FULL : 3 * FULL, :] = high[:FULL]
        block_cat[s, 3 * FULL : 3 * FULL + TAIL, :] = high[FULL:]
        block_cat[s, 3 * FULL + TAIL : 3 * FULL + 2 * TAIL, :] = low[FULL:]
        block_cat[s, 3 * FULL + 2 * TAIL : 3 * FULL + 3 * TAIL, :] = high[FULL:]
        block_cat[s, 3 * FULL + 3 * TAIL :, :] = jnp.zeros((128 - 3 * TAIL, LIST), BF16)
        block_grad[s] = jnp.zeros((D, LIST), F32)

    low_iota = lax.broadcasted_iota(jnp.int32, (128, 128), 0)
    high_iota = lax.broadcasted_iota(jnp.int32, (16, 128), 0)
    for g in range(groups):
        drawn = negatives[round_number, g]
        total = jnp.zeros((16, 128), F32)
        tail = tails[round_number, g].astype(F32)
        for b in range(GPAD // 128):
            row = drawn[b : b + 1, :]
            low_hot = jnp.where(low_iota == jnp.bitwise_and(row, 127), 1.0, 0.0).astype(BF16)
            high_hot = jnp.where(high_iota == jnp.right_shift(row, 7), 1.0, 0.0).astype(BF16)
            total = total + dot_nt(high_hot, low_hot)
            first = g * GPAD + 128 * b
            tail_columns[first : first + 128, :] = jnp.broadcast_to(tail[b : b + 1, :], (128, 128)).T
        bias[g] = jnp.where(total > 0.5, jnp.log2(jnp.maximum(total, 1.0)), -1e30)

    for stage in range(strips + 2):
        if stage < strips and stage % 2 == 0:
            for copy in load(stage // 2):
                copy.wait()
        if stage >= 3 and stage - 3 < strips - 2:
            for copy in store(stage - 3):
                copy.wait()

        @pl.loop(0, SUBS)
        def _(s):
            at = pl.ds(pl.multiple_of(s * LIST, LIST), LIST)
            if stage < strips:
                t = stage
                edges = slice((t % 2) * STRIP, (t % 2 + 1) * STRIP)
                scores[t % 2][:, at] = dot(cat[t // 2, edges, :], block_cat[s])
            if 2 <= stage:
                t = stage - 2
                edges = slice((t % 2) * STRIP, (t % 2 + 1) * STRIP)
                high = highs[t % 2][:, at]
                both = dot(flipped[t // 2, :, edges], high)
                cross = dot(flipped[t // 2, :D, edges], lows[t % 2][:, at])
                block_grad[s] += both[:D] + both[D:] + cross
            if 1 <= stage <= strips:
                t = stage - 1
                g = t // 2
                part = STRIP // SUBS
                row_iota = lax.broadcasted_iota(jnp.int32, (16, 1), 0)
                used = jnp.where(g < counts[0, round_number], GROUP, 0)
                for u in range(part // 16):
                    first = pl.multiple_of(s * part + u * 16, 16)
                    in_group = first + (t % 2) * STRIP
                    softmax_rows(
                        first,
                        g,
                        pl.ds(pl.multiple_of(in_group + g * GPAD, 16), 16),
                        jnp.where(row_iota + in_group < used, 1.0, 0.0),
                        scores[t % 2],
                        highs[t % 2],
                        lows[t % 2],
                        tail_columns,
                        bias,
                    )

        if 1 <= stage <= strips:
            for copy in store(stage - 1):
                copy.start()

    for t in (strips - 2, strips - 1):
        for copy in store(t):
            copy.wait()


def score_groups(round_number, group_counts, cat, flipped, block, tails, negatives):
    def kernel(*refs):
        score_kernel(round_number, *refs)

    groups = cat.shape[0]
    anywhere = pl.BlockSpec(memory_space=pl.ANY)
    return pl.pallas_call(
        kernel,
        in_specs=[SSPEC, anywhere, anywhere, VSPEC, VSPEC, VSPEC],
        out_specs=[anywhere, VSPEC],
        out_shape=[
            jax.ShapeDtypeStruct((groups, 2, GPAD, SLOTS), BF16),
            jax.ShapeDtypeStruct((SUBS, D, LIST), F32),
        ],
        scratch_shapes=[
            pltpu.VMEM(cat.shape, BF16),
            pltpu.VMEM(flipped.shape, BF16),
            pltpu.VMEM((SUBS, KCAT, LIST), BF16),
            pltpu.VMEM((STRIP, SLOTS), F32),
            pltpu.VMEM((STRIP, SLOTS), F32),
            pltpu.VMEM((STRIP, SLOTS), BF16),
            pltpu.VMEM((STRIP, SLOTS), BF16),
            pltpu.VMEM((STRIP, SLOTS), BF16),
            pltpu.VMEM((STRIP, SLOTS), BF16),
            pltpu.VMEM((groups * GPAD, 128), F32),
            pltpu.VMEM((groups, 16, 128), F32),
            pltpu.SemaphoreType.DMA((groups, 2)),
            pltpu.SemaphoreType.DMA((2, 2)),
        ],
        compiler_params=params(),
        cost_estimate=cost(40e9, 60e6),
        name="scores",
    )(group_counts, cat, flipped, block, tails, negatives)


def reduce_kernel(
    share_hbm, block, block_grad, own_share, packed,
    rows_high, rows_low, parts, from_mate, sums, relay_ahead, relay_behind, from_left, from_right,
    load_sems, mate_send, mate_recv, ring_send, ring_recv,
):
    me = lax.axis_index("sub")
    x = me // 2
    core = me % 2
    chips = SUBS // 2
    mate = x * 2 + (1 - core)
    right = ((x + 1) % chips) * 2 + core
    left = ((x + chips - 1) % chips) * 2 + core
    half = D // 2
    upper, lower = pl.ds(0, half), pl.ds(half, half)
    groups = share_hbm.shape[0]
    strips = groups * 2

    def block_of(k, c):
        return ((x + k) % chips) * 2 + c

    def load(t):
        slot = t % 2
        return pltpu.make_async_copy(
            share_hbm.at[t // 2, :, pl.ds(pl.multiple_of(slot * STRIP, STRIP), STRIP), :],
            parts.at[slot],
            load_sems.at[slot],
        )

    def to(device, source, target, send, recv, n):
        return pltpu.make_async_remote_copy(
            src_ref=source,
            dst_ref=target,
            send_sem=send.at[n],
            recv_sem=recv.at[n],
            device_id={"sub": device},
            device_id_type=pl.DeviceIdType.MESH,
        )

    load(0).start()
    barrier = pltpu.get_barrier_semaphore()
    for other in (mate, right, left):
        pl.semaphore_signal(
            barrier, inc=1, device_id={"sub": other}, device_id_type=pl.DeviceIdType.MESH
        )
    pl.semaphore_wait(barrier, 3)

    mates = {
        k: to(mate, block_grad.at[block_of(k, 1 - core)], from_mate.at[k], mate_send, mate_recv, k)
        for k in range(chips)
    }
    for k in (2, 1, 3, 0):
        mates[k].start()
    ring = (
        to(right, sums.at[2, upper], relay_ahead, ring_send, ring_recv, 0),
        to(left, sums.at[2, lower], relay_behind, ring_send, ring_recv, 1),
        to(right, sums.at[1, lower], from_left.at[lower], ring_send, ring_recv, 2),
        to(left, sums.at[3, upper], from_right.at[upper], ring_send, ring_recv, 3),
        to(right, sums.at[1, upper], from_left.at[upper], ring_send, ring_recv, 4),
        to(left, sums.at[3, lower], from_right.at[lower], ring_send, ring_recv, 5),
    )

    @pl.loop(0, SUBS)
    def _(s):
        for h in range(LIST // 128):
            rows = pl.ds(pl.multiple_of(s * LIST + h * 128, 128), 128)
            for j in range(4):
                lanes = slice(128 * h, 128 * (h + 1))
                if j < 3:
                    tile = block[s, 128 * j : 128 * (j + 1), lanes]
                else:
                    tile = jnp.concatenate(
                        [block[s, FULL:D, lanes], jnp.zeros((128 - TAIL, 128), F32)], axis=0
                    )
                high, low = split2(tile.T)
                rows_high[rows, 128 * j : 128 * (j + 1)] = high
                rows_low[rows, 128 * j : 128 * (j + 1)] = low

    def query_strip(t, more):
        if more:
            load(t + 1).start()
        load(t).wait()
        slot = t % 2
        for n in range(2):
            at = slice(256 * n, 256 * (n + 1))
            grad = (
                dot(parts[slot, 0], rows_high[:, at])
                + dot(parts[slot, 0], rows_low[:, at])
                + dot(parts[slot, 1], rows_high[:, at])
            )
            for h in range(2):
                for b in range(STRIP // 128):
                    packed[pl.ds(t * (4 * STRIP) + 512 * b + 2 * n + h, 128, stride=4), :] = grad[
                        128 * b : 128 * (b + 1), 128 * h : 128 * (h + 1)
                    ]

    def pair_sum(k):
        mates[k].wait()
        sums[k] = block_grad[block_of(k, core)] + from_mate[k]

    pair_sum(2)
    ring[0].start()
    ring[1].start()
    pair_sum(1)
    ring[2].start()
    pair_sum(3)
    ring[3].start()
    pair_sum(0)

    @pl.loop(0, 2)
    def _(t):
        query_strip(t, True)

    ring[0].wait()
    sums[1, upper, :] += relay_ahead[...]
    ring[4].start()
    ring[1].wait()
    sums[3, lower, :] += relay_behind[...]
    ring[5].start()

    @pl.loop(2, strips - 1)
    def _(t):
        query_strip(t, True)

    query_strip(strips - 1, False)

    for n in (2, 3, 4, 5):
        ring[n].wait()
    own_share[...] = sums[0] + from_left[...] + from_right[...]


def reduce_block(share, block, block_grad):
    groups = share.shape[0]
    return pl.pallas_call(
        reduce_kernel,
        in_specs=[pl.BlockSpec(memory_space=pl.ANY), VSPEC, VSPEC],
        out_specs=[VSPEC, VSPEC],
        out_shape=[
            jax.ShapeDtypeStruct((D, LIST), F32),
            jax.ShapeDtypeStruct((groups * GPAD * 4, 128), F32),
        ],
        scratch_shapes=[
            pltpu.VMEM((SLOTS, 512), BF16),
            pltpu.VMEM((SLOTS, 512), BF16),
            pltpu.VMEM((2, 2, STRIP, SLOTS), BF16),
            pltpu.VMEM((SUBS // 2, D, LIST), F32),
            pltpu.VMEM((SUBS // 2, D, LIST), F32),
            pltpu.VMEM((D // 2, LIST), F32),
            pltpu.VMEM((D // 2, LIST), F32),
            pltpu.VMEM((D, LIST), F32),
            pltpu.VMEM((D, LIST), F32),
            pltpu.SemaphoreType.DMA((2,)),
            pltpu.SemaphoreType.DMA((4,)),
            pltpu.SemaphoreType.DMA((4,)),
            pltpu.SemaphoreType.DMA((6,)),
            pltpu.SemaphoreType.DMA((6,)),
        ],
        compiler_params=params(collective_id=0, has_side_effects=True),
        cost_estimate=cost(20e9, 60e6),
        name="reduce_block",
    )(share, block, block_grad)


def head_kernel(round_number, counts, starts, packed, scale, out, *sums):
    g = pl.program_id(0)
    parts = len(sums)

    @pl.when(g == 0)
    def _():
        @pl.loop(0, sums[0].shape[0] // 128)
        def _(i):
            at = pl.ds(pl.multiple_of(i * 128, 128), 128)
            for part in sums:
                part[at, :] = jnp.zeros((128, 128), F32)

    @pl.when(g < counts[0, round_number])
    def _():
        base = (round_number * pl.num_programs(0) + g) * GROUP

        @pl.loop(0, GROUP // parts, unroll=2)
        def _(i):
            news = []
            for u in range(parts):
                e = i * parts + u
                row = pl.ds(pl.multiple_of(starts[base + e], 4), 4)
                at = pl.ds(pl.multiple_of(e * 4, 4), 4)
                term = packed[at, :] * scale[0, at, :]
                news.append((row, sums[u][row, :] + term))
            for u in range(parts):
                row, value = news[u]
                sums[u][row, :] = value

    @pl.when(g == pl.num_programs(0) - 1)
    def _():
        @pl.loop(0, out.shape[1] // 128)
        def _(i):
            columns = pl.ds(pl.multiple_of(i * 128, 128), 128)
            for j in range(4):
                at = pl.ds(i * 512 + j, 128, stride=4)
                tile = sums[0][at, :]
                for part in sums[1:]:
                    tile = tile + part[at, :]
                width = 128 if j < 3 else TAIL
                out[128 * j : 128 * j + width, columns] = tile.T[:width]


def head_gradients(round_number, group_counts, starts, packed, scale, rows):
    def kernel(*refs):
        head_kernel(round_number, *refs)

    groups = packed.shape[0] // (GPAD * 4)
    parts = 4
    return pl.pallas_call(
        kernel,
        grid=(groups,),
        in_specs=[
            SSPEC,
            SSPEC,
            pl.BlockSpec((GPAD * 4, 128), lambda g: (g, 0)),
            pl.BlockSpec((1, GROUP * 4, 128), lambda g: (round_number, g, 0)),
        ],
        out_specs=VSPEC,
        out_shape=jax.ShapeDtypeStruct((D, rows), F32),
        scratch_shapes=[pltpu.VMEM((rows * 4, 128), F32)] * parts,
        compiler_params=params(),
        cost_estimate=cost(2e9, 40e6),
        name="head_gradients",
    )(group_counts, starts, packed, scale)


def adagrad_kernel(
    round_number, last, counts, ids, head_grad, returned, table_t, state,
    new_table_t, new_state, *sent,
):
    rows = table_t.shape[1]
    width = 512
    listed = ids[round_number : round_number + 1, :].astype(F32)
    listed = jnp.broadcast_to(listed, (128, LIST)).T[:, 0:1]
    slot = lax.broadcasted_iota(jnp.int32, (LIST, 1), 0)
    wanted = jnp.where(slot < counts[0, round_number], listed, -1.0)
    high, mid, low = split3(returned[...])
    for first in range(0, rows, width):
        at = slice(first, first + width)
        row = (lax.broadcasted_iota(jnp.int32, (LIST, width), 1) + first).astype(F32)
        onehot = jnp.where(row == wanted, 1.0, 0.0).astype(BF16)
        totals = head_grad[:, at] + (dot(high, onehot) + dot(mid, onehot) + dot(low, onehot))
        fresh = state[:, at] + jnp.sum(totals * totals, axis=0, keepdims=True) / D
        new_state[:, at] = fresh
        new_table_t[:, at] = table_t[:, at] - LEARN_RATE * totals / jnp.sqrt(fresh)
    if not last:
        sent[0][...] = pick_columns(
            new_table_t[...], ids[round_number + 1 : round_number + 2, :], counts[0, round_number + 1]
        )


def adagrad(round_number, last, row_counts, row_lists, head_grad, returned, table_t, state):
    def kernel(*refs):
        adagrad_kernel(round_number, last, *refs)

    outs = [jax.ShapeDtypeStruct(table_t.shape, F32), jax.ShapeDtypeStruct(state.shape, F32)]
    if not last:
        outs.append(jax.ShapeDtypeStruct((D, LIST), F32))
    return pl.pallas_call(
        kernel,
        in_specs=[SSPEC] + [VSPEC] * 5,
        out_specs=[VSPEC] * len(outs),
        out_shape=outs,
        compiler_params=params(),
        name="adagrad",
    )(row_counts, row_lists, head_grad, returned, table_t, state)


def swap_partner(values, mask, beside, *operands):
    count = lax.axis_size("dom")

    def branch(m):
        route = [(i, i ^ m) for i in range(count)]
        return lambda held, *rest: (lax.ppermute(held, "dom", route), beside(*rest))

    return lax.switch(mask - 1, [branch(m) for m in range(1, count)], values, *operands)


def body(
    embeddings,
    adagrad_state,
    relations,
    pairing,
    row_lists,
    row_counts,
    group_counts,
    head_ids,
    relation_ids,
    tail_slots,
    negatives,
):
    rounds = pairing.shape[0]
    rows = embeddings.shape[0]
    groups = head_ids.shape[1] // GROUP
    table_t = embeddings.T
    row_counts = row_counts.T
    group_counts = group_counts.T
    state = adagrad_state.reshape(1, rows)

    def lanes(ids):
        ids = ids.reshape(rounds, groups, GROUP)
        ids = jnp.pad(ids, ((0, 0), (0, 0), (0, GPAD - GROUP)), constant_values=-1)
        return ids.reshape(rounds, groups, GPAD // 128, 128)

    tails = lanes(tail_slots)
    drawn = lanes(negatives)
    sent = first_sent(row_counts, row_lists, table_t)
    head_starts = head_ids.reshape(-1) * 4
    relation_starts = relation_ids.reshape(-1) * 4

    def first_queries(relation_starts, relations_t, head_starts, table_t):
        scale = gather_relations(relation_starts, relations_t, rounds)
        return scale, make_queries(0, head_starts, table_t, scale)

    for r in range(rounds):
        if r == 0:
            incoming, (scale, packed) = swap_partner(
                sent, pairing[r], first_queries, relation_starts, relations.T, head_starts, table_t
            )
        else:

            def later_queries(head_starts, table_t, scale):
                return make_queries(r, head_starts, table_t, scale)

            incoming, packed = swap_partner(
                sent, pairing[r], later_queries, head_starts, table_t, scale
            )
        block, cat, flipped = gather_block(incoming, packed)
        share, block_grad = score_groups(r, group_counts, cat, flipped, block, tails, drawn)
        own_share, packed = reduce_block(share, block, block_grad)

        def heads(counts, starts, packed, scale):
            return head_gradients(r, counts, starts, packed, scale, rows)

        returned, head_grad = swap_partner(
            own_share, pairing[r], heads, group_counts, head_starts, packed, scale
        )
        last = r == rounds - 1
        done = adagrad(r, last, row_counts, row_lists, head_grad, returned, table_t, state)
        table_t, state = done[0], done[1]
        if not last:
            sent = done[2]
    return (table_t.T, state.reshape(rows))


def solution(mesh):
    in_specs = (
        P(("dom", "sub"), None),
        P(("dom", "sub")),
        P(),
        P(),
        P(None, ("dom", "sub")),
        P(None, ("dom", "sub")),
        P(None, ("dom", "sub")),
        P(None, ("dom", "sub")),
        P(None, ("dom", "sub")),
        P(None, ("dom", "sub")),
        P(None, ("dom", "sub")),
    )
    out_specs = (P(("dom", "sub"), None), P(("dom", "sub")))
    return jax.shard_map(body, mesh=mesh, in_specs=in_specs, out_specs=out_specs, check_vma=False)
```

```python
import jax
import jax.numpy as jnp
from jax import lax
from jax.experimental import pallas as pl
from jax.experimental.pallas import tpu as pltpu
from jax.sharding import PartitionSpec as P

F32 = jnp.float32
BF16 = jnp.bfloat16
LOG2E = 1.4426950408889634
LEARN_RATE = 0.1

D = 400
FULL = 384
TAIL = D - FULL
GROUP = 1000
GPAD = 1024
LIST = 256
SUBS = 8
SLOTS = SUBS * LIST
STRIP = GPAD // 2
KCAT = 3 * FULL + 128
VMEM_LIMIT = 60 * 1024 * 1024

VSPEC = pl.BlockSpec(memory_space=pltpu.VMEM)
SSPEC = pl.BlockSpec(memory_space=pltpu.SMEM)
ANYSPEC = pl.BlockSpec(memory_space=pl.ANY)
UNROLL = 20


def split2(x):
    high = x.astype(BF16)
    return high, (x - high.astype(F32)).astype(BF16)


def split3(x):
    high, rest = split2(x)
    low = x - high.astype(F32) - rest.astype(F32)
    return high, rest, low.astype(BF16)


def dot(a, b):
    return lax.dot_general(a, b, (((1,), (0,)), ((), ())), preferred_element_type=F32)


def dot_nt(a, b):
    return lax.dot_general(a, b, (((1,), (1,)), ((), ())), preferred_element_type=F32)


def params(**more):
    return pltpu.CompilerParams(vmem_limit_bytes=VMEM_LIMIT, **more)


def cost(flops, moved):
    return pl.CostEstimate(flops=int(flops), bytes_accessed=int(moved), transcendentals=0)


def pack_rows(source, target, start, target_start):
    for j in range(4):
        if j < 3:
            tile = source[128 * j : 128 * (j + 1), pl.ds(start, 128)]
        else:
            tile = jnp.concatenate(
                [source[FULL:D, pl.ds(start, 128)], jnp.zeros((128 - TAIL, 128), F32)], axis=0
            )
        target[pl.ds(target_start + j, 128, stride=4), :] = tile.T


def relation_kernel(ids, table_hbm, out_hbm, table_t, packed, rows, load_sems, store_sems):
    pieces = load_sems.shape[0]
    width = table_hbm.shape[1] // pieces
    chunks = store_sems.shape[0]
    each = ids.shape[0] // chunks
    per_round = chunks // out_hbm.shape[0]

    def load(i):
        part = pl.ds(pl.multiple_of(i * width, 128), width)
        return pltpu.make_async_copy(table_hbm.at[:, part], table_t.at[:, part], load_sems.at[i])

    def store(c):
        return pltpu.make_async_copy(
            rows.at[pl.ds(pl.multiple_of(c * each * 4, 8), each * 4), :],
            out_hbm.at[c // per_round, pl.ds(pl.multiple_of(c % per_round * each * 4, 8), each * 4), :],
            store_sems.at[c],
        )

    for i in range(pieces):
        load(i).start()

    @pl.loop(0, pieces)
    def _(i):
        load(i).wait()

        @pl.loop(0, width // 128)
        def _(tile):
            start = pl.multiple_of(i * width + tile * 128, 128)
            pack_rows(table_t, packed, start, start * 4)

    @pl.loop(0, chunks)
    def _(c):
        @pl.loop(0, each // UNROLL)
        def _(i):
            first = c * each + i * UNROLL
            for u in range(UNROLL):
                row = pl.multiple_of(ids[first + u], 4)
                at = pl.multiple_of(first * 4 + 4 * u, 4)
                rows[pl.ds(at, 4), :] = packed[pl.ds(row, 4), :]

        store(c).start()

    for c in range(chunks):
        store(c).wait()


def gather_relations(starts, relations_t, rounds):
    count = relations_t.shape[1]
    edges = starts.shape[0] // rounds
    return pl.pallas_call(
        relation_kernel,
        in_specs=[SSPEC, ANYSPEC],
        out_specs=ANYSPEC,
        out_shape=jax.ShapeDtypeStruct((rounds, edges * 4, 128), F32),
        scratch_shapes=[
            pltpu.VMEM(relations_t.shape, F32),
            pltpu.VMEM((count * 4, 128), F32),
            pltpu.VMEM((rounds * edges * 4, 128), F32),
            pltpu.SemaphoreType.DMA((2,)),
            pltpu.SemaphoreType.DMA((rounds * edges // GROUP,)),
        ],
        compiler_params=params(),
        cost_estimate=cost(2e9, 60e6),
        name="relation_rows",
    )(starts, relations_t)


def pick_columns(table_t, ids_row, count):
    rows = table_t.shape[1]
    slot = lax.broadcasted_iota(jnp.int32, ids_row.shape, 1)
    wanted = jnp.where(slot < count, ids_row, -1)
    row = lax.broadcasted_iota(jnp.int32, (rows, LIST), 0)
    onehot = jnp.where(row == wanted, 1.0, 0.0).astype(BF16)
    high, mid, low = split3(table_t)
    return dot(high, onehot) + dot(mid, onehot) + dot(low, onehot)


def sent_kernel(counts, ids, table_t, out):
    out[...] = pick_columns(table_t[...], ids[0:1, :], counts[0, 0])


def first_sent(row_counts, row_lists, table_t):
    return pl.pallas_call(
        sent_kernel,
        in_specs=[SSPEC, VSPEC, VSPEC],
        out_specs=VSPEC,
        out_shape=jax.ShapeDtypeStruct((D, LIST), F32),
        compiler_params=params(),
        name="sent_rows",
    )(row_counts, row_lists, table_t)


def query_kernel(round_number, starts, table_t, scale, packed, table):
    g = pl.program_id(0)

    @pl.when(g == 0)
    def _():
        @pl.loop(0, table_t.shape[1] // 128)
        def _(i):
            start = pl.multiple_of(i * 128, 128)
            pack_rows(table_t, table, start, start * 4)

    base = (round_number * pl.num_programs(0) + g) * GROUP

    @pl.loop(0, GROUP // UNROLL)
    def _(i):
        for u in range(UNROLL):
            row = pl.ds(pl.multiple_of(starts[base + i * UNROLL + u], 4), 4)
            at = pl.ds(pl.multiple_of(i * (4 * UNROLL) + 4 * u, 4), 4)
            packed[at, :] = table[row, :] * scale[0, at, :]

    packed[4 * GROUP :, :] = jnp.zeros((4 * (GPAD - GROUP), 128), F32)


def make_queries(round_number, starts, table_t, scale):
    def kernel(*refs):
        query_kernel(round_number, *refs)

    groups = scale.shape[1] // (4 * GROUP)
    return pl.pallas_call(
        kernel,
        grid=(groups,),
        in_specs=[
            SSPEC,
            VSPEC,
            pl.BlockSpec((1, GROUP * 4, 128), lambda g: (round_number, g, 0)),
        ],
        out_specs=pl.BlockSpec((GPAD * 4, 128), lambda g: (g, 0)),
        out_shape=jax.ShapeDtypeStruct((groups * GPAD * 4, 128), F32),
        scratch_shapes=[pltpu.VMEM((table_t.shape[1] * 4, 128), F32)],
        compiler_params=params(),
        cost_estimate=cost(2e9, 20e6),
        name="queries",
    )(starts, table_t, scale)


def gather_kernel(
    own, packed_hbm, block, cat_hbm, flipped_hbm,
    packed, cat, flipped, own_sem, load_sems, cat_sems, flipped_sems,
    ring_send, ring_recv, mate_send, mate_recv,
):
    me = lax.axis_index("sub")
    x = me // 2
    core = me % 2
    chips = SUBS // 2
    mate = x * 2 + (1 - core)
    right = ((x + 1) % chips) * 2 + core
    left = ((x + chips - 1) % chips) * 2 + core
    across = ((x + 2) % chips) * 2 + core
    half = D // 2
    upper, lower = pl.ds(0, half), pl.ds(half, half)
    groups = cat.shape[0]
    rows_of = GPAD * 4

    def to(device, source, target, send, recv, n):
        return pltpu.make_async_remote_copy(
            src_ref=source,
            dst_ref=target,
            send_sem=send.at[n],
            recv_sem=recv.at[n],
            device_id={"sub": device},
            device_id_type=pl.DeviceIdType.MESH,
        )

    def load(g):
        return pltpu.make_async_copy(
            packed_hbm.at[pl.ds(g * rows_of, rows_of), :],
            packed.at[pl.ds(g * rows_of, rows_of), :],
            load_sems.at[g],
        )

    def store(g):
        return (
            pltpu.make_async_copy(cat.at[g], cat_hbm.at[g], cat_sems.at[g]),
            pltpu.make_async_copy(flipped.at[g], flipped_hbm.at[g], flipped_sems.at[g]),
        )

    for g in range(groups):
        load(g).start()
    keep = pltpu.make_async_copy(own, block.at[me], own_sem)
    keep.start()

    barrier = pltpu.get_barrier_semaphore()
    for other in (mate, right, left):
        pl.semaphore_signal(
            barrier, inc=1, device_id={"sub": other}, device_id_type=pl.DeviceIdType.MESH
        )
    pl.semaphore_wait(barrier, 3)

    ring = (
        to(right, own.at[upper], block.at[me, upper], ring_send, ring_recv, 0),
        to(left, own.at[lower], block.at[me, lower], ring_send, ring_recv, 1),
        to(right, own.at[lower], block.at[me, lower], ring_send, ring_recv, 2),
        to(left, own.at[upper], block.at[me, upper], ring_send, ring_recv, 3),
        to(right, block.at[left, upper], block.at[left, upper], ring_send, ring_recv, 4),
        to(left, block.at[right, lower], block.at[right, lower], ring_send, ring_recv, 5),
    )
    landed = (
        (left, upper),
        (right, lower),
        (left, lower),
        (right, upper),
        (across, upper),
        (across, lower),
    )
    own_to_mate = to(mate, own, block.at[me], mate_send, mate_recv, 6)
    to_mate = [
        to(mate, block.at[owner, part], block.at[owner, part], mate_send, mate_recv, n)
        for n, (owner, part) in enumerate(landed)
    ]

    for n in range(4):
        ring[n].start()
    own_to_mate.start()

    def operands(g):
        load(g).wait()

        @pl.loop(0, GPAD // 128)
        def _(b):
            rows = pl.ds(pl.multiple_of(b * 128, 128), 128)
            for j in range(4):
                tile = packed[pl.ds(g * rows_of + b * 512 + j, 128, stride=4), :]
                high, low = split2(tile * LOG2E)
                if j < 3:
                    cat[g, rows, 128 * j : 128 * (j + 1)] = high
                    cat[g, rows, FULL + 128 * j : FULL + 128 * (j + 1)] = high
                    cat[g, rows, 2 * FULL + 128 * j : 2 * FULL + 128 * (j + 1)] = low
                else:
                    high, low = high.astype(F32), low.astype(F32)
                    both = high + pltpu.roll(high, TAIL, 1) + pltpu.roll(low, 2 * TAIL, 1)
                    cat[g, rows, 3 * FULL :] = both.astype(BF16)
                high, low = split2(tile.T)
                width = 128 if j < 3 else TAIL
                flipped[g, 128 * j : 128 * j + width, rows] = high[:width]
                flipped[g, D + 128 * j : D + 128 * j + width, rows] = low[:width]

        for copy in store(g):
            copy.start()

    def pass_on(n):
        ring[n].wait_recv()
        if n < 2:
            ring[4 + n].start()
        to_mate[n].start()

    operands(0)
    pass_on(0)
    pass_on(1)
    operands(1)
    pass_on(2)
    pass_on(3)
    operands(2)
    pass_on(4)
    pass_on(5)
    for copy in ring:
        copy.wait_send()
    own_to_mate.wait()
    for copy in to_mate:
        copy.wait()
    keep.wait()
    for g in range(groups):
        for copy in store(g):
            copy.wait()


def gather_block(own, packed):
    groups = packed.shape[0] // (4 * GPAD)
    dma = pltpu.SemaphoreType.DMA
    shapes = [
        jax.ShapeDtypeStruct((SUBS, D, LIST), F32),
        jax.ShapeDtypeStruct((groups, GPAD, KCAT), BF16),
        jax.ShapeDtypeStruct((groups, 2 * D, GPAD), BF16),
    ]
    return pl.pallas_call(
        gather_kernel,
        in_specs=[ANYSPEC, ANYSPEC],
        out_specs=[ANYSPEC] * 3,
        out_shape=shapes,
        scratch_shapes=[
            pltpu.VMEM(packed.shape, F32),
            pltpu.VMEM(shapes[1].shape, BF16),
            pltpu.VMEM(shapes[2].shape, BF16),
            dma,
            dma((groups,)),
            dma((groups,)),
            dma((groups,)),
            dma((6,)),
            dma((6,)),
            dma((7,)),
            dma((7,)),
        ],
        compiler_params=params(collective_id=1, has_side_effects=True),
        cost_estimate=cost(2e9, 40e6),
        name="gather_block",
    )(own, packed)


def softmax_rows(first, group, active_rows, active, scores, share_high, share_low, tail_columns, bias):
    count = 16
    rows = pl.ds(first, count)
    tiles = SLOTS // 128
    lane = lax.broadcasted_iota(jnp.int32, (count, 128), 1).astype(F32)
    offset = tail_columns[active_rows, :] - lane
    own = None
    shifted = []
    top = None
    for j in range(tiles):
        raw = scores[rows, 128 * j : 128 * (j + 1)]
        hit = jnp.where(offset == 128.0 * j, raw, 0.0)
        own = hit if own is None else own + hit
        moved = raw + bias[group, j : j + 1, :]
        shifted.append(moved)
        top = moved if top is None else jnp.maximum(top, moved)
    positive = jnp.sum(own, axis=1, keepdims=True)
    top = jnp.maximum(jnp.max(top, axis=1, keepdims=True), positive)
    total = None
    weights = []
    for j in range(tiles):
        weight = jnp.exp2(shifted[j] - top)
        weights.append(weight)
        total = weight if total is None else total + weight
    negative_sum = jnp.sum(total, axis=1, keepdims=True)
    inverse = active / (jnp.exp2(positive - top) + negative_sum)
    own_share = -negative_sum * inverse
    for j in range(tiles):
        value = weights[j] * inverse + jnp.where(offset == 128.0 * j, own_share, 0.0)
        high, low = split2(value)
        share_high[rows, 128 * j : 128 * (j + 1)] = high
        share_low[rows, 128 * j : 128 * (j + 1)] = low


def score_kernel(
    round_number, counts, cat_hbm, flipped_hbm, block, tails, negatives, share_hbm, block_grad,
    cat, flipped, block_cat, scores_a, scores_b, high_a, high_b, low_a, low_b, tail_columns, bias,
    in_sems, out_sems,
):
    groups = cat.shape[0]
    strips = groups * 2
    scores = (scores_a, scores_b)
    highs = (high_a, high_b)
    lows = (low_a, low_b)

    def load(g):
        return (
            pltpu.make_async_copy(cat_hbm.at[g], cat.at[g], in_sems.at[g, 0]),
            pltpu.make_async_copy(flipped_hbm.at[g], flipped.at[g], in_sems.at[g, 1]),
        )

    def store(t):
        target = pl.ds((t % 2) * STRIP, STRIP)
        return (
            pltpu.make_async_copy(highs[t % 2], share_hbm.at[t // 2, 0, target, :], out_sems.at[t % 2, 0]),
            pltpu.make_async_copy(lows[t % 2], share_hbm.at[t // 2, 1, target, :], out_sems.at[t % 2, 1]),
        )

    for g in range(groups):
        for copy in load(g):
            copy.start()

    @pl.loop(0, SUBS)
    def _(s):
        high, low = split2(block[s])
        block_cat[s, 0:FULL, :] = high[:FULL]
        block_cat[s, FULL : 2 * FULL, :] = low[:FULL]
        block_cat[s, 2 * FULL : 3 * FULL, :] = high[:FULL]
        block_cat[s, 3 * FULL : 3 * FULL + TAIL, :] = high[FULL:]
        block_cat[s, 3 * FULL + TAIL : 3 * FULL + 2 * TAIL, :] = low[FULL:]
        block_cat[s, 3 * FULL + 2 * TAIL : 3 * FULL + 3 * TAIL, :] = high[FULL:]
        block_cat[s, 3 * FULL + 3 * TAIL :, :] = jnp.zeros((128 - 3 * TAIL, LIST), BF16)
        block_grad[s] = jnp.zeros((D, LIST), F32)

    low_iota = lax.broadcasted_iota(jnp.int32, (128, 128), 0)
    high_iota = lax.broadcasted_iota(jnp.int32, (16, 128), 0)
    for g in range(groups):
        drawn = negatives[round_number, g]
        total = jnp.zeros((16, 128), F32)
        tail = tails[round_number, g].astype(F32)
        for b in range(GPAD // 128):
            row = drawn[b : b + 1, :]
            low_hot = jnp.where(low_iota == jnp.bitwise_and(row, 127), 1.0, 0.0).astype(BF16)
            high_hot = jnp.where(high_iota == jnp.right_shift(row, 7), 1.0, 0.0).astype(BF16)
            total = total + dot_nt(high_hot, low_hot)
            first = g * GPAD + 128 * b
            tail_columns[first : first + 128, :] = jnp.broadcast_to(tail[b : b + 1, :], (128, 128)).T
        bias[g] = jnp.where(total > 0.5, jnp.log2(jnp.maximum(total, 1.0)), -1e30)

    for stage in range(strips + 2):
        if stage < strips and stage % 2 == 0:
            for copy in load(stage // 2):
                copy.wait()
        if stage >= 3 and stage - 3 < strips - 2:
            for copy in store(stage - 3):
                copy.wait()

        @pl.loop(0, SUBS)
        def _(s):
            at = pl.ds(pl.multiple_of(s * LIST, LIST), LIST)
            if stage < strips:
                t = stage
                edges = slice((t % 2) * STRIP, (t % 2 + 1) * STRIP)
                scores[t % 2][:, at] = dot(cat[t // 2, edges, :], block_cat[s])
            if 2 <= stage:
                t = stage - 2
                edges = slice((t % 2) * STRIP, (t % 2 + 1) * STRIP)
                high = highs[t % 2][:, at]
                both = dot(flipped[t // 2, :, edges], high)
                cross = dot(flipped[t // 2, :D, edges], lows[t % 2][:, at])
                block_grad[s] += both[:D] + both[D:] + cross
            if 1 <= stage <= strips:
                t = stage - 1
                g = t // 2
                part = STRIP // SUBS
                row_iota = lax.broadcasted_iota(jnp.int32, (16, 1), 0)
                used = jnp.where(g < counts[0, round_number], GROUP, 0)
                for u in range(part // 16):
                    first = pl.multiple_of(s * part + u * 16, 16)
                    in_group = first + (t % 2) * STRIP
                    softmax_rows(
                        first,
                        g,
                        pl.ds(pl.multiple_of(in_group + g * GPAD, 16), 16),
                        jnp.where(row_iota + in_group < used, 1.0, 0.0),
                        scores[t % 2],
                        highs[t % 2],
                        lows[t % 2],
                        tail_columns,
                        bias,
                    )

        if 1 <= stage <= strips:
            for copy in store(stage - 1):
                copy.start()

    for t in (strips - 2, strips - 1):
        for copy in store(t):
            copy.wait()


def score_groups(round_number, group_counts, cat, flipped, block, tails, negatives):
    def kernel(*refs):
        score_kernel(round_number, *refs)

    groups = cat.shape[0]
    anywhere = pl.BlockSpec(memory_space=pl.ANY)
    return pl.pallas_call(
        kernel,
        in_specs=[SSPEC, anywhere, anywhere, VSPEC, VSPEC, VSPEC],
        out_specs=[anywhere, VSPEC],
        out_shape=[
            jax.ShapeDtypeStruct((groups, 2, GPAD, SLOTS), BF16),
            jax.ShapeDtypeStruct((SUBS, D, LIST), F32),
        ],
        scratch_shapes=[
            pltpu.VMEM(cat.shape, BF16),
            pltpu.VMEM(flipped.shape, BF16),
            pltpu.VMEM((SUBS, KCAT, LIST), BF16),
            pltpu.VMEM((STRIP, SLOTS), F32),
            pltpu.VMEM((STRIP, SLOTS), F32),
            pltpu.VMEM((STRIP, SLOTS), BF16),
            pltpu.VMEM((STRIP, SLOTS), BF16),
            pltpu.VMEM((STRIP, SLOTS), BF16),
            pltpu.VMEM((STRIP, SLOTS), BF16),
            pltpu.VMEM((groups * GPAD, 128), F32),
            pltpu.VMEM((groups, 16, 128), F32),
            pltpu.SemaphoreType.DMA((groups, 2)),
            pltpu.SemaphoreType.DMA((2, 2)),
        ],
        compiler_params=params(),
        cost_estimate=cost(40e9, 60e6),
        name="scores",
    )(group_counts, cat, flipped, block, tails, negatives)


def reduce_kernel(
    share_hbm, block, block_grad, own_share, packed_hbm,
    packed, rows_high, rows_low, parts, from_mate, sums, relay_ahead, relay_behind, from_left, from_right,
    load_sems, store_sems, mate_send, mate_recv, ring_send, ring_recv,
):
    me = lax.axis_index("sub")
    x = me // 2
    core = me % 2
    chips = SUBS // 2
    mate = x * 2 + (1 - core)
    right = ((x + 1) % chips) * 2 + core
    left = ((x + chips - 1) % chips) * 2 + core
    half = D // 2
    upper, lower = pl.ds(0, half), pl.ds(half, half)
    groups = share_hbm.shape[0]
    strips = groups * 2

    def block_of(k, c):
        return ((x + k) % chips) * 2 + c

    def load(t):
        slot = t % 2
        return pltpu.make_async_copy(
            share_hbm.at[t // 2, :, pl.ds(pl.multiple_of(slot * STRIP, STRIP), STRIP), :],
            parts.at[slot],
            load_sems.at[slot],
        )

    def store(t):
        part = pl.ds(pl.multiple_of(t * (4 * STRIP), 8), 4 * STRIP)
        return pltpu.make_async_copy(packed.at[part, :], packed_hbm.at[part, :], store_sems.at[t])

    def to(device, source, target, send, recv, n):
        return pltpu.make_async_remote_copy(
            src_ref=source,
            dst_ref=target,
            send_sem=send.at[n],
            recv_sem=recv.at[n],
            device_id={"sub": device},
            device_id_type=pl.DeviceIdType.MESH,
        )

    load(0).start()
    barrier = pltpu.get_barrier_semaphore()
    for other in (mate, right, left):
        pl.semaphore_signal(
            barrier, inc=1, device_id={"sub": other}, device_id_type=pl.DeviceIdType.MESH
        )
    pl.semaphore_wait(barrier, 3)

    mates = {
        k: to(mate, block_grad.at[block_of(k, 1 - core)], from_mate.at[k], mate_send, mate_recv, k)
        for k in range(chips)
    }
    for k in (2, 1, 3, 0):
        mates[k].start()
    ring = (
        to(right, sums.at[2, upper], relay_ahead, ring_send, ring_recv, 0),
        to(left, sums.at[2, lower], relay_behind, ring_send, ring_recv, 1),
        to(right, sums.at[1, lower], from_left.at[lower], ring_send, ring_recv, 2),
        to(left, sums.at[3, upper], from_right.at[upper], ring_send, ring_recv, 3),
        to(right, sums.at[1, upper], from_left.at[upper], ring_send, ring_recv, 4),
        to(left, sums.at[3, lower], from_right.at[lower], ring_send, ring_recv, 5),
    )

    @pl.loop(0, SUBS)
    def _(s):
        for h in range(LIST // 128):
            rows = pl.ds(pl.multiple_of(s * LIST + h * 128, 128), 128)
            for j in range(4):
                lanes = slice(128 * h, 128 * (h + 1))
                if j < 3:
                    tile = block[s, 128 * j : 128 * (j + 1), lanes]
                else:
                    tile = jnp.concatenate(
                        [block[s, FULL:D, lanes], jnp.zeros((128 - TAIL, 128), F32)], axis=0
                    )
                high, low = split2(tile.T)
                rows_high[rows, 128 * j : 128 * (j + 1)] = high
                rows_low[rows, 128 * j : 128 * (j + 1)] = low

    def query_strip(t, more):
        if more:
            load(t + 1).start()
        load(t).wait()
        slot = t % 2
        for n in range(2):
            at = slice(256 * n, 256 * (n + 1))
            grad = (
                dot(parts[slot, 0], rows_high[:, at])
                + dot(parts[slot, 0], rows_low[:, at])
                + dot(parts[slot, 1], rows_high[:, at])
            )
            for h in range(2):
                for b in range(STRIP // 128):
                    packed[pl.ds(t * (4 * STRIP) + 512 * b + 2 * n + h, 128, stride=4), :] = grad[
                        128 * b : 128 * (b + 1), 128 * h : 128 * (h + 1)
                    ]
        store(t).start()

    def pair_sum(k):
        mates[k].wait()
        sums[k] = block_grad[block_of(k, core)] + from_mate[k]

    pair_sum(2)
    ring[0].start()
    ring[1].start()
    pair_sum(1)
    ring[2].start()
    pair_sum(3)
    ring[3].start()
    pair_sum(0)

    @pl.loop(0, 2)
    def _(t):
        query_strip(t, True)

    ring[0].wait()
    sums[1, upper, :] += relay_ahead[...]
    ring[4].start()
    ring[1].wait()
    sums[3, lower, :] += relay_behind[...]
    ring[5].start()

    @pl.loop(2, strips - 1)
    def _(t):
        query_strip(t, True)

    query_strip(strips - 1, False)

    for n in (2, 3, 4, 5):
        ring[n].wait()
    own_share[...] = sums[0] + from_left[...] + from_right[...]
    for t in range(strips):
        store(t).wait()


def reduce_block(share, block, block_grad):
    groups = share.shape[0]
    return pl.pallas_call(
        reduce_kernel,
        in_specs=[pl.BlockSpec(memory_space=pl.ANY), VSPEC, VSPEC],
        out_specs=[VSPEC, ANYSPEC],
        out_shape=[
            jax.ShapeDtypeStruct((D, LIST), F32),
            jax.ShapeDtypeStruct((groups * GPAD * 4, 128), F32),
        ],
        scratch_shapes=[
            pltpu.VMEM((groups * GPAD * 4, 128), F32),
            pltpu.VMEM((SLOTS, 512), BF16),
            pltpu.VMEM((SLOTS, 512), BF16),
            pltpu.VMEM((2, 2, STRIP, SLOTS), BF16),
            pltpu.VMEM((SUBS // 2, D, LIST), F32),
            pltpu.VMEM((SUBS // 2, D, LIST), F32),
            pltpu.VMEM((D // 2, LIST), F32),
            pltpu.VMEM((D // 2, LIST), F32),
            pltpu.VMEM((D, LIST), F32),
            pltpu.VMEM((D, LIST), F32),
            pltpu.SemaphoreType.DMA((2,)),
            pltpu.SemaphoreType.DMA((groups * 2,)),
            pltpu.SemaphoreType.DMA((4,)),
            pltpu.SemaphoreType.DMA((4,)),
            pltpu.SemaphoreType.DMA((6,)),
            pltpu.SemaphoreType.DMA((6,)),
        ],
        compiler_params=params(collective_id=0, has_side_effects=True),
        cost_estimate=cost(20e9, 60e6),
        name="reduce_block",
    )(share, block, block_grad)


def head_kernel(round_number, counts, starts, packed, scale, out, *sums):
    g = pl.program_id(0)
    parts = len(sums)

    @pl.when(g == 0)
    def _():
        @pl.loop(0, sums[0].shape[0] // 128)
        def _(i):
            at = pl.ds(pl.multiple_of(i * 128, 128), 128)
            for part in sums:
                part[at, :] = jnp.zeros((128, 128), F32)

    @pl.when(g < counts[0, round_number])
    def _():
        base = (round_number * pl.num_programs(0) + g) * GROUP

        @pl.loop(0, GROUP // parts, unroll=2)
        def _(i):
            news = []
            for u in range(parts):
                e = i * parts + u
                row = pl.ds(pl.multiple_of(starts[base + e], 4), 4)
                at = pl.ds(pl.multiple_of(e * 4, 4), 4)
                term = packed[at, :] * scale[0, at, :]
                news.append((row, sums[u][row, :] + term))
            for u in range(parts):
                row, value = news[u]
                sums[u][row, :] = value

    @pl.when(g == pl.num_programs(0) - 1)
    def _():
        @pl.loop(0, out.shape[1] // 128)
        def _(i):
            columns = pl.ds(pl.multiple_of(i * 128, 128), 128)
            for j in range(4):
                at = pl.ds(i * 512 + j, 128, stride=4)
                tile = sums[0][at, :]
                for part in sums[1:]:
                    tile = tile + part[at, :]
                width = 128 if j < 3 else TAIL
                out[128 * j : 128 * j + width, columns] = tile.T[:width]


def head_gradients(round_number, group_counts, starts, packed, scale, rows):
    def kernel(*refs):
        head_kernel(round_number, *refs)

    groups = packed.shape[0] // (GPAD * 4)
    parts = 4
    return pl.pallas_call(
        kernel,
        grid=(groups,),
        in_specs=[
            SSPEC,
            SSPEC,
            pl.BlockSpec((GPAD * 4, 128), lambda g: (g, 0)),
            pl.BlockSpec((1, GROUP * 4, 128), lambda g: (round_number, g, 0)),
        ],
        out_specs=VSPEC,
        out_shape=jax.ShapeDtypeStruct((D, rows), F32),
        scratch_shapes=[pltpu.VMEM((rows * 4, 128), F32)] * parts,
        compiler_params=params(),
        cost_estimate=cost(2e9, 40e6),
        name="head_gradients",
    )(group_counts, starts, packed, scale)


def adagrad_kernel(
    round_number, last, counts, ids, head_grad, returned, table_t, state,
    new_table_t, new_state, *sent,
):
    rows = table_t.shape[1]
    width = 512
    listed = ids[round_number : round_number + 1, :].astype(F32)
    listed = jnp.broadcast_to(listed, (128, LIST)).T[:, 0:1]
    slot = lax.broadcasted_iota(jnp.int32, (LIST, 1), 0)
    wanted = jnp.where(slot < counts[0, round_number], listed, -1.0)
    high, mid, low = split3(returned[...])
    for first in range(0, rows, width):
        at = slice(first, first + width)
        row = (lax.broadcasted_iota(jnp.int32, (LIST, width), 1) + first).astype(F32)
        onehot = jnp.where(row == wanted, 1.0, 0.0).astype(BF16)
        totals = head_grad[:, at] + (dot(high, onehot) + dot(mid, onehot) + dot(low, onehot))
        fresh = state[:, at] + jnp.sum(totals * totals, axis=0, keepdims=True) / D
        new_state[:, at] = fresh
        new_table_t[:, at] = table_t[:, at] - totals * (LEARN_RATE / jnp.sqrt(fresh))
    if not last:
        sent[0][...] = pick_columns(
            new_table_t[...], ids[round_number + 1 : round_number + 2, :], counts[0, round_number + 1]
        )


def adagrad(round_number, last, row_counts, row_lists, head_grad, returned, table_t, state):
    def kernel(*refs):
        adagrad_kernel(round_number, last, *refs)

    outs = [jax.ShapeDtypeStruct(table_t.shape, F32), jax.ShapeDtypeStruct(state.shape, F32)]
    if not last:
        outs.append(jax.ShapeDtypeStruct((D, LIST), F32))
    return pl.pallas_call(
        kernel,
        in_specs=[SSPEC] + [VSPEC] * 5,
        out_specs=[VSPEC] * len(outs),
        out_shape=outs,
        compiler_params=params(),
        name="adagrad",
    )(row_counts, row_lists, head_grad, returned, table_t, state)


def swap_partner(values, mask, beside, *operands):
    count = lax.axis_size("dom")

    def branch(m):
        route = [(i, i ^ m) for i in range(count)]
        return lambda held, *rest: (lax.ppermute(held, "dom", route), beside(*rest))

    return lax.switch(mask - 1, [branch(m) for m in range(1, count)], values, *operands)


def body(
    embeddings,
    adagrad_state,
    relations,
    pairing,
    row_lists,
    row_counts,
    group_counts,
    head_ids,
    relation_ids,
    tail_slots,
    negatives,
):
    rounds = pairing.shape[0]
    rows = embeddings.shape[0]
    groups = head_ids.shape[1] // GROUP
    table_t = embeddings.T
    row_counts = row_counts.T
    group_counts = group_counts.T
    state = adagrad_state.reshape(1, rows)

    def lanes(ids):
        ids = ids.reshape(rounds, groups, GROUP)
        ids = jnp.pad(ids, ((0, 0), (0, 0), (0, GPAD - GROUP)), constant_values=-1)
        return ids.reshape(rounds, groups, GPAD // 128, 128)

    tails = lanes(tail_slots)
    drawn = lanes(negatives)
    sent = first_sent(row_counts, row_lists, table_t)
    head_starts = head_ids.reshape(-1) * 4
    relation_starts = relation_ids.reshape(-1) * 4

    def first_queries(relation_starts, relations_t, head_starts, table_t):
        scale = gather_relations(relation_starts, relations_t, rounds)
        return scale, make_queries(0, head_starts, table_t, scale)

    for r in range(rounds):
        if r == 0:
            incoming, (scale, packed) = swap_partner(
                sent, pairing[r], first_queries, relation_starts, relations.T, head_starts, table_t
            )
        else:

            def later_queries(head_starts, table_t, scale):
                return make_queries(r, head_starts, table_t, scale)

            incoming, packed = swap_partner(
                sent, pairing[r], later_queries, head_starts, table_t, scale
            )
        block, cat, flipped = gather_block(incoming, packed)
        share, block_grad = score_groups(r, group_counts, cat, flipped, block, tails, drawn)
        own_share, packed = reduce_block(share, block, block_grad)

        def heads(counts, starts, packed, scale):
            return head_gradients(r, counts, starts, packed, scale, rows)

        returned, head_grad = swap_partner(
            own_share, pairing[r], heads, group_counts, head_starts, packed, scale
        )
        last = r == rounds - 1
        done = adagrad(r, last, row_counts, row_lists, head_grad, returned, table_t, state)
        table_t, state = done[0], done[1]
        if not last:
            sent = done[2]
    return (table_t.T, state.reshape(rows))


def solution(mesh):
    in_specs = (
        P(("dom", "sub"), None),
        P(("dom", "sub")),
        P(),
        P(),
        P(None, ("dom", "sub")),
        P(None, ("dom", "sub")),
        P(None, ("dom", "sub")),
        P(None, ("dom", "sub")),
        P(None, ("dom", "sub")),
        P(None, ("dom", "sub")),
        P(None, ("dom", "sub")),
    )
    out_specs = (P(("dom", "sub"), None), P(("dom", "sub")))
    return jax.shard_map(body, mesh=mesh, in_specs=in_specs, out_specs=out_specs, check_vma=False)
```

```python
import jax
import jax.numpy as jnp
from jax import lax
from jax.experimental import pallas as pl
from jax.experimental.pallas import tpu as pltpu
from jax.sharding import PartitionSpec as P

F32 = jnp.float32
BF16 = jnp.bfloat16
LOG2E = 1.4426950408889634
LEARN_RATE = 0.1

D = 400
FULL = 384
TAIL = D - FULL
GROUP = 1000
GPAD = 1024
LIST = 256
SUBS = 8
SLOTS = SUBS * LIST
STRIP = GPAD // 2
KCAT = 3 * FULL + 128
VMEM_LIMIT = 60 * 1024 * 1024

VSPEC = pl.BlockSpec(memory_space=pltpu.VMEM)
SSPEC = pl.BlockSpec(memory_space=pltpu.SMEM)
ANYSPEC = pl.BlockSpec(memory_space=pl.ANY)
UNROLL = 20


def split2(x):
    high = x.astype(BF16)
    return high, (x - high.astype(F32)).astype(BF16)


def split3(x):
    high, rest = split2(x)
    low = x - high.astype(F32) - rest.astype(F32)
    return high, rest, low.astype(BF16)


def dot(a, b):
    return lax.dot_general(a, b, (((1,), (0,)), ((), ())), preferred_element_type=F32)


def dot_nt(a, b):
    return lax.dot_general(a, b, (((1,), (1,)), ((), ())), preferred_element_type=F32)


def params(**more):
    return pltpu.CompilerParams(vmem_limit_bytes=VMEM_LIMIT, **more)


def cost(flops, moved):
    return pl.CostEstimate(flops=int(flops), bytes_accessed=int(moved), transcendentals=0)


def pack_rows(source, target, start, target_start):
    for j in range(4):
        if j < 3:
            tile = source[128 * j : 128 * (j + 1), pl.ds(start, 128)]
        else:
            tile = jnp.concatenate(
                [source[FULL:D, pl.ds(start, 128)], jnp.zeros((128 - TAIL, 128), F32)], axis=0
            )
        target[pl.ds(target_start + j, 128, stride=4), :] = tile.T


def relation_kernel(ids, table_hbm, out_hbm, table_t, packed, rows, load_sems, store_sems):
    pieces = load_sems.shape[0]
    width = table_hbm.shape[1] // pieces
    chunks = store_sems.shape[0]
    each = ids.shape[0] // chunks
    per_round = chunks // out_hbm.shape[0]

    def load(i):
        part = pl.ds(pl.multiple_of(i * width, 128), width)
        return pltpu.make_async_copy(table_hbm.at[:, part], table_t.at[:, part], load_sems.at[i])

    def store(c):
        return pltpu.make_async_copy(
            rows.at[pl.ds(pl.multiple_of(c * each * 4, 8), each * 4), :],
            out_hbm.at[c // per_round, pl.ds(pl.multiple_of(c % per_round * each * 4, 8), each * 4), :],
            store_sems.at[c],
        )

    for i in range(pieces):
        load(i).start()

    @pl.loop(0, pieces)
    def _(i):
        load(i).wait()

        @pl.loop(0, width // 128)
        def _(tile):
            start = pl.multiple_of(i * width + tile * 128, 128)
            pack_rows(table_t, packed, start, start * 4)

    @pl.loop(0, chunks)
    def _(c):
        @pl.loop(0, each // (2 * UNROLL))
        def _(i):
            first = c * each + i * (2 * UNROLL)
            for u in range(2 * UNROLL):
                row = pl.multiple_of(ids[first + u], 4)
                at = pl.multiple_of(first * 4 + 4 * u, 4)
                rows[pl.ds(at, 4), :] = packed[pl.ds(row, 4), :]

        store(c).start()

    for c in range(chunks):
        store(c).wait()


def gather_relations(starts, relations_t, rounds):
    count = relations_t.shape[1]
    edges = starts.shape[0] // rounds
    return pl.pallas_call(
        relation_kernel,
        in_specs=[SSPEC, ANYSPEC],
        out_specs=ANYSPEC,
        out_shape=jax.ShapeDtypeStruct((rounds, edges * 4, 128), F32),
        scratch_shapes=[
            pltpu.VMEM(relations_t.shape, F32),
            pltpu.VMEM((count * 4, 128), F32),
            pltpu.VMEM((rounds * edges * 4, 128), F32),
            pltpu.SemaphoreType.DMA((2,)),
            pltpu.SemaphoreType.DMA((rounds * edges // GROUP,)),
        ],
        compiler_params=params(),
        cost_estimate=cost(2e9, 60e6),
        name="relation_rows",
    )(starts, relations_t)


def pick_columns(table_t, ids_row, count):
    rows = table_t.shape[1]
    slot = lax.broadcasted_iota(jnp.int32, ids_row.shape, 1)
    wanted = jnp.where(slot < count, ids_row, -1)
    row = lax.broadcasted_iota(jnp.int32, (rows, LIST), 0)
    onehot = jnp.where(row == wanted, 1.0, 0.0).astype(BF16)
    high, mid, low = split3(table_t)
    return dot(high, onehot) + dot(mid, onehot) + dot(low, onehot)


def sent_kernel(counts, ids, table_t, out):
    out[...] = pick_columns(table_t[...], ids[0:1, :], counts[0, 0])


def first_sent(row_counts, row_lists, table_t):
    return pl.pallas_call(
        sent_kernel,
        in_specs=[SSPEC, VSPEC, VSPEC],
        out_specs=VSPEC,
        out_shape=jax.ShapeDtypeStruct((D, LIST), F32),
        compiler_params=params(),
        name="sent_rows",
    )(row_counts, row_lists, table_t)


def query_kernel(round_number, starts, table_t, scale, packed, table):
    g = pl.program_id(0)

    @pl.when(g == 0)
    def _():
        @pl.loop(0, table_t.shape[1] // 128)
        def _(i):
            start = pl.multiple_of(i * 128, 128)
            pack_rows(table_t, table, start, start * 4)

    base = (round_number * pl.num_programs(0) + g) * GROUP

    @pl.loop(0, GROUP // UNROLL)
    def _(i):
        for u in range(UNROLL):
            row = pl.ds(pl.multiple_of(starts[base + i * UNROLL + u], 4), 4)
            at = pl.ds(pl.multiple_of(i * (4 * UNROLL) + 4 * u, 4), 4)
            packed[at, :] = table[row, :] * scale[0, at, :]

    packed[4 * GROUP :, :] = jnp.zeros((4 * (GPAD - GROUP), 128), F32)


def make_queries(round_number, starts, table_t, scale):
    def kernel(*refs):
        query_kernel(round_number, *refs)

    groups = scale.shape[1] // (4 * GROUP)
    return pl.pallas_call(
        kernel,
        grid=(groups,),
        in_specs=[
            SSPEC,
            VSPEC,
            pl.BlockSpec((1, GROUP * 4, 128), lambda g: (round_number, g, 0)),
        ],
        out_specs=pl.BlockSpec((GPAD * 4, 128), lambda g: (g, 0)),
        out_shape=jax.ShapeDtypeStruct((groups * GPAD * 4, 128), F32),
        scratch_shapes=[pltpu.VMEM((table_t.shape[1] * 4, 128), F32)],
        compiler_params=params(),
        cost_estimate=cost(2e9, 20e6),
        name="queries",
    )(starts, table_t, scale)


def gather_kernel(
    own, packed_hbm, block, cat_hbm, flipped_hbm,
    packed, cat, flipped, own_sem, load_sems, cat_sems, flipped_sems,
    ring_send, ring_recv, mate_send, mate_recv,
):
    me = lax.axis_index("sub")
    x = me // 2
    core = me % 2
    chips = SUBS // 2
    mate = x * 2 + (1 - core)
    right = ((x + 1) % chips) * 2 + core
    left = ((x + chips - 1) % chips) * 2 + core
    across = ((x + 2) % chips) * 2 + core
    half = D // 2
    upper, lower = pl.ds(0, half), pl.ds(half, half)
    groups = cat.shape[0]
    rows_of = GPAD * 4

    def to(device, source, target, send, recv, n):
        return pltpu.make_async_remote_copy(
            src_ref=source,
            dst_ref=target,
            send_sem=send.at[n],
            recv_sem=recv.at[n],
            device_id={"sub": device},
            device_id_type=pl.DeviceIdType.MESH,
        )

    def load(g):
        return pltpu.make_async_copy(
            packed_hbm.at[pl.ds(g * rows_of, rows_of), :],
            packed.at[pl.ds(g * rows_of, rows_of), :],
            load_sems.at[g],
        )

    def store(g):
        return (
            pltpu.make_async_copy(cat.at[g], cat_hbm.at[g], cat_sems.at[g]),
            pltpu.make_async_copy(flipped.at[g], flipped_hbm.at[g], flipped_sems.at[g]),
        )

    for g in range(groups):
        load(g).start()
    keep = pltpu.make_async_copy(own, block.at[me], own_sem)
    keep.start()

    barrier = pltpu.get_barrier_semaphore()
    for other in (mate, right, left):
        pl.semaphore_signal(
            barrier, inc=1, device_id={"sub": other}, device_id_type=pl.DeviceIdType.MESH
        )
    pl.semaphore_wait(barrier, 3)

    ring = (
        to(right, own.at[upper], block.at[me, upper], ring_send, ring_recv, 0),
        to(left, own.at[lower], block.at[me, lower], ring_send, ring_recv, 1),
        to(right, own.at[lower], block.at[me, lower], ring_send, ring_recv, 2),
        to(left, own.at[upper], block.at[me, upper], ring_send, ring_recv, 3),
        to(right, block.at[left, upper], block.at[left, upper], ring_send, ring_recv, 4),
        to(left, block.at[right, lower], block.at[right, lower], ring_send, ring_recv, 5),
    )
    landed = (
        (left, upper),
        (right, lower),
        (left, lower),
        (right, upper),
        (across, upper),
        (across, lower),
    )
    own_to_mate = to(mate, own, block.at[me], mate_send, mate_recv, 6)
    to_mate = [
        to(mate, block.at[owner, part], block.at[owner, part], mate_send, mate_recv, n)
        for n, (owner, part) in enumerate(landed)
    ]

    for n in range(4):
        ring[n].start()
    own_to_mate.start()

    def operands(g):
        load(g).wait()

        @pl.loop(0, GPAD // 128)
        def _(b):
            rows = pl.ds(pl.multiple_of(b * 128, 128), 128)
            for j in range(4):
                tile = packed[pl.ds(g * rows_of + b * 512 + j, 128, stride=4), :]
                high, low = split2(tile * LOG2E)
                if j < 3:
                    cat[g, rows, 128 * j : 128 * (j + 1)] = high
                    cat[g, rows, FULL + 128 * j : FULL + 128 * (j + 1)] = high
                    cat[g, rows, 2 * FULL + 128 * j : 2 * FULL + 128 * (j + 1)] = low
                else:
                    high, low = high.astype(F32), low.astype(F32)
                    both = high + pltpu.roll(high, TAIL, 1) + pltpu.roll(low, 2 * TAIL, 1)
                    cat[g, rows, 3 * FULL :] = both.astype(BF16)
                high, low = split2(tile.T)
                width = 128 if j < 3 else TAIL
                flipped[g, 128 * j : 128 * j + width, rows] = high[:width]
                flipped[g, D + 128 * j : D + 128 * j + width, rows] = low[:width]

        for copy in store(g):
            copy.start()

    def pass_on(n):
        ring[n].wait_recv()
        if n < 2:
            ring[4 + n].start()
        to_mate[n].start()

    operands(0)
    pass_on(0)
    pass_on(1)
    operands(1)
    pass_on(2)
    pass_on(3)
    operands(2)
    pass_on(4)
    pass_on(5)
    for copy in ring:
        copy.wait_send()
    own_to_mate.wait()
    for copy in to_mate:
        copy.wait()
    keep.wait()
    for g in range(groups):
        for copy in store(g):
            copy.wait()


def gather_block(own, packed):
    groups = packed.shape[0] // (4 * GPAD)
    dma = pltpu.SemaphoreType.DMA
    shapes = [
        jax.ShapeDtypeStruct((SUBS, D, LIST), F32),
        jax.ShapeDtypeStruct((groups, GPAD, KCAT), BF16),
        jax.ShapeDtypeStruct((groups, 2 * D, GPAD), BF16),
    ]
    return pl.pallas_call(
        gather_kernel,
        in_specs=[ANYSPEC, ANYSPEC],
        out_specs=[ANYSPEC] * 3,
        out_shape=shapes,
        scratch_shapes=[
            pltpu.VMEM(packed.shape, F32),
            pltpu.VMEM(shapes[1].shape, BF16),
            pltpu.VMEM(shapes[2].shape, BF16),
            dma,
            dma((groups,)),
            dma((groups,)),
            dma((groups,)),
            dma((6,)),
            dma((6,)),
            dma((7,)),
            dma((7,)),
        ],
        compiler_params=params(collective_id=1, has_side_effects=True),
        cost_estimate=cost(2e9, 40e6),
        name="gather_block",
    )(own, packed)


def softmax_rows(first, group, active_rows, active, scores, share_high, share_low, tail_columns, bias):
    count = 16
    rows = pl.ds(first, count)
    tiles = SLOTS // 128
    lane = lax.broadcasted_iota(jnp.int32, (count, 128), 1).astype(F32)
    offset = tail_columns[active_rows, :] - lane
    own = None
    shifted = []
    top = None
    for j in range(tiles):
        raw = scores[rows, 128 * j : 128 * (j + 1)]
        hit = jnp.where(offset == 128.0 * j, raw, 0.0)
        own = hit if own is None else own + hit
        moved = raw + bias[group, j : j + 1, :]
        shifted.append(moved)
        top = moved if top is None else jnp.maximum(top, moved)
    positive = jnp.sum(own, axis=1, keepdims=True)
    top = jnp.maximum(jnp.max(top, axis=1, keepdims=True), positive)
    total = None
    weights = []
    for j in range(tiles):
        weight = jnp.exp2(shifted[j] - top)
        weights.append(weight)
        total = weight if total is None else total + weight
    negative_sum = jnp.sum(total, axis=1, keepdims=True)
    inverse = active / (jnp.exp2(positive - top) + negative_sum)
    own_share = -negative_sum * inverse
    for j in range(tiles):
        value = weights[j] * inverse + jnp.where(offset == 128.0 * j, own_share, 0.0)
        high, low = split2(value)
        share_high[rows, 128 * j : 128 * (j + 1)] = high
        share_low[rows, 128 * j : 128 * (j + 1)] = low


def score_kernel(
    round_number, counts, cat_hbm, flipped_hbm, block, tails, negatives, share_hbm, block_grad,
    cat, flipped, block_cat, scores_a, scores_b, high_a, high_b, low_a, low_b, tail_columns, bias,
    in_sems, out_sems,
):
    groups = cat.shape[0]
    strips = groups * 2
    scores = (scores_a, scores_b)
    highs = (high_a, high_b)
    lows = (low_a, low_b)

    def load(g):
        return (
            pltpu.make_async_copy(cat_hbm.at[g], cat.at[g], in_sems.at[g, 0]),
            pltpu.make_async_copy(flipped_hbm.at[g], flipped.at[g], in_sems.at[g, 1]),
        )

    def store(t):
        target = pl.ds((t % 2) * STRIP, STRIP)
        return (
            pltpu.make_async_copy(highs[t % 2], share_hbm.at[t // 2, 0, target, :], out_sems.at[t % 2, 0]),
            pltpu.make_async_copy(lows[t % 2], share_hbm.at[t // 2, 1, target, :], out_sems.at[t % 2, 1]),
        )

    for g in range(groups):
        for copy in load(g):
            copy.start()

    @pl.loop(0, SUBS)
    def _(s):
        high, low = split2(block[s])
        block_cat[s, 0:FULL, :] = high[:FULL]
        block_cat[s, FULL : 2 * FULL, :] = low[:FULL]
        block_cat[s, 2 * FULL : 3 * FULL, :] = high[:FULL]
        block_cat[s, 3 * FULL : 3 * FULL + TAIL, :] = high[FULL:]
        block_cat[s, 3 * FULL + TAIL : 3 * FULL + 2 * TAIL, :] = low[FULL:]
        block_cat[s, 3 * FULL + 2 * TAIL : 3 * FULL + 3 * TAIL, :] = high[FULL:]
        block_cat[s, 3 * FULL + 3 * TAIL :, :] = jnp.zeros((128 - 3 * TAIL, LIST), BF16)
        block_grad[s] = jnp.zeros((D, LIST), F32)

    low_iota = lax.broadcasted_iota(jnp.int32, (128, 128), 0)
    high_iota = lax.broadcasted_iota(jnp.int32, (16, 128), 0)
    for g in range(groups):
        drawn = negatives[round_number, g]
        total = jnp.zeros((16, 128), F32)
        tail = tails[round_number, g].astype(F32)
        for b in range(GPAD // 128):
            row = drawn[b : b + 1, :]
            low_hot = jnp.where(low_iota == jnp.bitwise_and(row, 127), 1.0, 0.0).astype(BF16)
            high_hot = jnp.where(high_iota == jnp.right_shift(row, 7), 1.0, 0.0).astype(BF16)
            total = total + dot_nt(high_hot, low_hot)
            first = g * GPAD + 128 * b
            tail_columns[first : first + 128, :] = jnp.broadcast_to(tail[b : b + 1, :], (128, 128)).T
        bias[g] = jnp.where(total > 0.5, jnp.log2(jnp.maximum(total, 1.0)), -1e30)

    for stage in range(strips + 2):
        if stage < strips and stage % 2 == 0:
            for copy in load(stage // 2):
                copy.wait()
        if stage >= 3 and stage - 3 < strips - 2:
            for copy in store(stage - 3):
                copy.wait()

        @pl.loop(0, SUBS)
        def _(s):
            at = pl.ds(pl.multiple_of(s * LIST, LIST), LIST)
            if stage < strips:
                t = stage
                edges = slice((t % 2) * STRIP, (t % 2 + 1) * STRIP)
                scores[t % 2][:, at] = dot(cat[t // 2, edges, :], block_cat[s])
            if 2 <= stage:
                t = stage - 2
                edges = slice((t % 2) * STRIP, (t % 2 + 1) * STRIP)
                high = highs[t % 2][:, at]
                both = dot(flipped[t // 2, :, edges], high)
                cross = dot(flipped[t // 2, :D, edges], lows[t % 2][:, at])
                block_grad[s] += both[:D] + both[D:] + cross
            if 1 <= stage <= strips:
                t = stage - 1
                g = t // 2
                part = STRIP // SUBS
                row_iota = lax.broadcasted_iota(jnp.int32, (16, 1), 0)
                used = jnp.where(g < counts[0, round_number], GROUP, 0)
                for u in range(part // 16):
                    first = pl.multiple_of(s * part + u * 16, 16)
                    in_group = first + (t % 2) * STRIP
                    softmax_rows(
                        first,
                        g,
                        pl.ds(pl.multiple_of(in_group + g * GPAD, 16), 16),
                        jnp.where(row_iota + in_group < used, 1.0, 0.0),
                        scores[t % 2],
                        highs[t % 2],
                        lows[t % 2],
                        tail_columns,
                        bias,
                    )

        if 1 <= stage <= strips:
            for copy in store(stage - 1):
                copy.start()

    for t in (strips - 2, strips - 1):
        for copy in store(t):
            copy.wait()


def score_groups(round_number, group_counts, cat, flipped, block, tails, negatives):
    def kernel(*refs):
        score_kernel(round_number, *refs)

    groups = cat.shape[0]
    anywhere = pl.BlockSpec(memory_space=pl.ANY)
    return pl.pallas_call(
        kernel,
        in_specs=[SSPEC, anywhere, anywhere, VSPEC, VSPEC, VSPEC],
        out_specs=[anywhere, VSPEC],
        out_shape=[
            jax.ShapeDtypeStruct((groups, 2, GPAD, SLOTS), BF16),
            jax.ShapeDtypeStruct((SUBS, D, LIST), F32),
        ],
        scratch_shapes=[
            pltpu.VMEM(cat.shape, BF16),
            pltpu.VMEM(flipped.shape, BF16),
            pltpu.VMEM((SUBS, KCAT, LIST), BF16),
            pltpu.VMEM((STRIP, SLOTS), F32),
            pltpu.VMEM((STRIP, SLOTS), F32),
            pltpu.VMEM((STRIP, SLOTS), BF16),
            pltpu.VMEM((STRIP, SLOTS), BF16),
            pltpu.VMEM((STRIP, SLOTS), BF16),
            pltpu.VMEM((STRIP, SLOTS), BF16),
            pltpu.VMEM((groups * GPAD, 128), F32),
            pltpu.VMEM((groups, 16, 128), F32),
            pltpu.SemaphoreType.DMA((groups, 2)),
            pltpu.SemaphoreType.DMA((2, 2)),
        ],
        compiler_params=params(),
        cost_estimate=cost(40e9, 60e6),
        name="scores",
    )(group_counts, cat, flipped, block, tails, negatives)


def reduce_kernel(
    share_hbm, block, block_grad, own_share, packed_hbm,
    packed, rows_high, rows_low, parts, from_mate, sums, relay_ahead, relay_behind, from_left, from_right,
    load_sems, store_sems, mate_send, mate_recv, ring_send, ring_recv,
):
    me = lax.axis_index("sub")
    x = me // 2
    core = me % 2
    chips = SUBS // 2
    mate = x * 2 + (1 - core)
    right = ((x + 1) % chips) * 2 + core
    left = ((x + chips - 1) % chips) * 2 + core
    half = D // 2
    upper, lower = pl.ds(0, half), pl.ds(half, half)
    groups = share_hbm.shape[0]
    strips = groups * 2

    def block_of(k, c):
        return ((x + k) % chips) * 2 + c

    def load(t):
        slot = t % 2
        return pltpu.make_async_copy(
            share_hbm.at[t // 2, :, pl.ds(pl.multiple_of(slot * STRIP, STRIP), STRIP), :],
            parts.at[slot],
            load_sems.at[slot],
        )

    def store(t):
        part = pl.ds(pl.multiple_of(t * (4 * STRIP), 8), 4 * STRIP)
        return pltpu.make_async_copy(packed.at[part, :], packed_hbm.at[part, :], store_sems.at[t])

    def to(device, source, target, send, recv, n):
        return pltpu.make_async_remote_copy(
            src_ref=source,
            dst_ref=target,
            send_sem=send.at[n],
            recv_sem=recv.at[n],
            device_id={"sub": device},
            device_id_type=pl.DeviceIdType.MESH,
        )

    load(0).start()
    barrier = pltpu.get_barrier_semaphore()
    for other in (mate, right, left):
        pl.semaphore_signal(
            barrier, inc=1, device_id={"sub": other}, device_id_type=pl.DeviceIdType.MESH
        )
    pl.semaphore_wait(barrier, 3)

    mates = {
        k: to(mate, block_grad.at[block_of(k, 1 - core)], from_mate.at[k], mate_send, mate_recv, k)
        for k in range(chips)
    }
    for k in (2, 1, 3, 0):
        mates[k].start()
    ring = (
        to(right, sums.at[2, upper], relay_ahead, ring_send, ring_recv, 0),
        to(left, sums.at[2, lower], relay_behind, ring_send, ring_recv, 1),
        to(right, sums.at[1, lower], from_left.at[lower], ring_send, ring_recv, 2),
        to(left, sums.at[3, upper], from_right.at[upper], ring_send, ring_recv, 3),
        to(right, sums.at[1, upper], from_left.at[upper], ring_send, ring_recv, 4),
        to(left, sums.at[3, lower], from_right.at[lower], ring_send, ring_recv, 5),
    )

    @pl.loop(0, SUBS)
    def _(s):
        for h in range(LIST // 128):
            rows = pl.ds(pl.multiple_of(s * LIST + h * 128, 128), 128)
            for j in range(4):
                lanes = slice(128 * h, 128 * (h + 1))
                if j < 3:
                    tile = block[s, 128 * j : 128 * (j + 1), lanes]
                else:
                    tile = jnp.concatenate(
                        [block[s, FULL:D, lanes], jnp.zeros((128 - TAIL, 128), F32)], axis=0
                    )
                high, low = split2(tile.T)
                rows_high[rows, 128 * j : 128 * (j + 1)] = high
                rows_low[rows, 128 * j : 128 * (j + 1)] = low

    def query_strip(t, more):
        if more:
            load(t + 1).start()
        load(t).wait()
        slot = t % 2
        for n in range(2):
            at = slice(256 * n, 256 * (n + 1))
            grad = (
                dot(parts[slot, 0], rows_high[:, at])
                + dot(parts[slot, 0], rows_low[:, at])
                + dot(parts[slot, 1], rows_high[:, at])
            )
            for h in range(2):
                for b in range(STRIP // 128):
                    packed[pl.ds(t * (4 * STRIP) + 512 * b + 2 * n + h, 128, stride=4), :] = grad[
                        128 * b : 128 * (b + 1), 128 * h : 128 * (h + 1)
                    ]
        store(t).start()

    def pair_sum(k):
        mates[k].wait()
        sums[k] = block_grad[block_of(k, core)] + from_mate[k]

    pair_sum(2)
    ring[0].start()
    ring[1].start()
    pair_sum(1)
    ring[2].start()
    pair_sum(3)
    ring[3].start()
    pair_sum(0)

    @pl.loop(0, 2)
    def _(t):
        query_strip(t, True)

    ring[0].wait()
    sums[1, upper, :] += relay_ahead[...]
    ring[4].start()
    ring[1].wait()
    sums[3, lower, :] += relay_behind[...]
    ring[5].start()

    @pl.loop(2, strips - 1)
    def _(t):
        query_strip(t, True)

    query_strip(strips - 1, False)

    for n in (2, 3, 4, 5):
        ring[n].wait()
    own_share[...] = sums[0] + from_left[...] + from_right[...]
    for t in range(strips):
        store(t).wait()


def reduce_block(share, block, block_grad):
    groups = share.shape[0]
    return pl.pallas_call(
        reduce_kernel,
        in_specs=[pl.BlockSpec(memory_space=pl.ANY), VSPEC, VSPEC],
        out_specs=[VSPEC, ANYSPEC],
        out_shape=[
            jax.ShapeDtypeStruct((D, LIST), F32),
            jax.ShapeDtypeStruct((groups * GPAD * 4, 128), F32),
        ],
        scratch_shapes=[
            pltpu.VMEM((groups * GPAD * 4, 128), F32),
            pltpu.VMEM((SLOTS, 512), BF16),
            pltpu.VMEM((SLOTS, 512), BF16),
            pltpu.VMEM((2, 2, STRIP, SLOTS), BF16),
            pltpu.VMEM((SUBS // 2, D, LIST), F32),
            pltpu.VMEM((SUBS // 2, D, LIST), F32),
            pltpu.VMEM((D // 2, LIST), F32),
            pltpu.VMEM((D // 2, LIST), F32),
            pltpu.VMEM((D, LIST), F32),
            pltpu.VMEM((D, LIST), F32),
            pltpu.SemaphoreType.DMA((2,)),
            pltpu.SemaphoreType.DMA((groups * 2,)),
            pltpu.SemaphoreType.DMA((4,)),
            pltpu.SemaphoreType.DMA((4,)),
            pltpu.SemaphoreType.DMA((6,)),
            pltpu.SemaphoreType.DMA((6,)),
        ],
        compiler_params=params(collective_id=0, has_side_effects=True),
        cost_estimate=cost(20e9, 60e6),
        name="reduce_block",
    )(share, block, block_grad)


def head_kernel(round_number, counts, starts, packed, scale, out, *sums):
    g = pl.program_id(0)
    parts = len(sums)

    @pl.when(g == 0)
    def _():
        @pl.loop(0, sums[0].shape[0] // 128)
        def _(i):
            at = pl.ds(pl.multiple_of(i * 128, 128), 128)
            for part in sums:
                part[at, :] = jnp.zeros((128, 128), F32)

    @pl.when(g < counts[0, round_number])
    def _():
        base = (round_number * pl.num_programs(0) + g) * GROUP

        @pl.loop(0, GROUP // parts, unroll=2)
        def _(i):
            news = []
            for u in range(parts):
                e = i * parts + u
                row = pl.ds(pl.multiple_of(starts[base + e], 4), 4)
                at = pl.ds(pl.multiple_of(e * 4, 4), 4)
                term = packed[at, :] * scale[0, at, :]
                news.append((row, sums[u][row, :] + term))
            for u in range(parts):
                row, value = news[u]
                sums[u][row, :] = value

    @pl.when(g == pl.num_programs(0) - 1)
    def _():
        @pl.loop(0, out.shape[1] // 128)
        def _(i):
            columns = pl.ds(pl.multiple_of(i * 128, 128), 128)
            for j in range(4):
                at = pl.ds(i * 512 + j, 128, stride=4)
                tile = sums[0][at, :]
                for part in sums[1:]:
                    tile = tile + part[at, :]
                width = 128 if j < 3 else TAIL
                out[128 * j : 128 * j + width, columns] = tile.T[:width]


def head_gradients(round_number, group_counts, starts, packed, scale, rows):
    def kernel(*refs):
        head_kernel(round_number, *refs)

    groups = packed.shape[0] // (GPAD * 4)
    parts = 4
    return pl.pallas_call(
        kernel,
        grid=(groups,),
        in_specs=[
            SSPEC,
            SSPEC,
            pl.BlockSpec((GPAD * 4, 128), lambda g: (g, 0)),
            pl.BlockSpec((1, GROUP * 4, 128), lambda g: (round_number, g, 0)),
        ],
        out_specs=VSPEC,
        out_shape=jax.ShapeDtypeStruct((D, rows), F32),
        scratch_shapes=[pltpu.VMEM((rows * 4, 128), F32)] * parts,
        compiler_params=params(),
        cost_estimate=cost(2e9, 40e6),
        name="head_gradients",
    )(group_counts, starts, packed, scale)


def adagrad_kernel(
    round_number, last, counts, ids, head_grad, returned, table_t, state,
    new_table_t, new_state, *sent,
):
    rows = table_t.shape[1]
    width = 512
    listed = ids[round_number : round_number + 1, :].astype(F32)
    listed = jnp.broadcast_to(listed, (128, LIST)).T[:, 0:1]
    slot = lax.broadcasted_iota(jnp.int32, (LIST, 1), 0)
    wanted = jnp.where(slot < counts[0, round_number], listed, -1.0)
    high, mid, low = split3(returned[...])
    for first in range(0, rows, width):
        at = slice(first, first + width)
        row = (lax.broadcasted_iota(jnp.int32, (LIST, width), 1) + first).astype(F32)
        onehot = jnp.where(row == wanted, 1.0, 0.0).astype(BF16)
        totals = head_grad[:, at] + (dot(high, onehot) + dot(mid, onehot) + dot(low, onehot))
        fresh = state[:, at] + jnp.sum(totals * totals, axis=0, keepdims=True) / D
        new_state[:, at] = fresh
        new_table_t[:, at] = table_t[:, at] - totals * (LEARN_RATE / jnp.sqrt(fresh))
    if not last:
        sent[0][...] = pick_columns(
            new_table_t[...], ids[round_number + 1 : round_number + 2, :], counts[0, round_number + 1]
        )


def adagrad(round_number, last, row_counts, row_lists, head_grad, returned, table_t, state):
    def kernel(*refs):
        adagrad_kernel(round_number, last, *refs)

    outs = [jax.ShapeDtypeStruct(table_t.shape, F32), jax.ShapeDtypeStruct(state.shape, F32)]
    if not last:
        outs.append(jax.ShapeDtypeStruct((D, LIST), F32))
    return pl.pallas_call(
        kernel,
        in_specs=[SSPEC] + [VSPEC] * 5,
        out_specs=[VSPEC] * len(outs),
        out_shape=outs,
        compiler_params=params(),
        name="adagrad",
    )(row_counts, row_lists, head_grad, returned, table_t, state)


def swap_partner(values, mask, beside, *operands):
    count = lax.axis_size("dom")

    def branch(m):
        route = [(i, i ^ m) for i in range(count)]
        return lambda held, *rest: (lax.ppermute(held, "dom", route), beside(*rest))

    return lax.switch(mask - 1, [branch(m) for m in range(1, count)], values, *operands)


def body(
    embeddings,
    adagrad_state,
    relations,
    pairing,
    row_lists,
    row_counts,
    group_counts,
    head_ids,
    relation_ids,
    tail_slots,
    negatives,
):
    rounds = pairing.shape[0]
    rows = embeddings.shape[0]
    groups = head_ids.shape[1] // GROUP
    table_t = embeddings.T
    row_counts = row_counts.T
    group_counts = group_counts.T
    state = adagrad_state.reshape(1, rows)

    def lanes(ids):
        ids = ids.reshape(rounds, groups, GROUP)
        ids = jnp.pad(ids, ((0, 0), (0, 0), (0, GPAD - GROUP)), constant_values=-1)
        return ids.reshape(rounds, groups, GPAD // 128, 128)

    tails = lanes(tail_slots)
    drawn = lanes(negatives)
    sent = first_sent(row_counts, row_lists, table_t)
    head_starts = head_ids.reshape(-1) * 4
    relation_starts = relation_ids.reshape(-1) * 4

    def first_queries(relation_starts, relations_t, head_starts, table_t):
        scale = gather_relations(relation_starts, relations_t, rounds)
        return scale, make_queries(0, head_starts, table_t, scale)

    for r in range(rounds):
        if r == 0:
            incoming, (scale, packed) = swap_partner(
                sent, pairing[r], first_queries, relation_starts, relations.T, head_starts, table_t
            )
        else:

            def later_queries(head_starts, table_t, scale):
                return make_queries(r, head_starts, table_t, scale)

            incoming, packed = swap_partner(
                sent, pairing[r], later_queries, head_starts, table_t, scale
            )
        block, cat, flipped = gather_block(incoming, packed)
        share, block_grad = score_groups(r, group_counts, cat, flipped, block, tails, drawn)
        own_share, packed = reduce_block(share, block, block_grad)

        def heads(counts, starts, packed, scale):
            return head_gradients(r, counts, starts, packed, scale, rows)

        returned, head_grad = swap_partner(
            own_share, pairing[r], heads, group_counts, head_starts, packed, scale
        )
        last = r == rounds - 1
        done = adagrad(r, last, row_counts, row_lists, head_grad, returned, table_t, state)
        table_t, state = done[0], done[1]
        if not last:
            sent = done[2]
    return (table_t.T, state.reshape(rows))


def solution(mesh):
    in_specs = (
        P(("dom", "sub"), None),
        P(("dom", "sub")),
        P(),
        P(),
        P(None, ("dom", "sub")),
        P(None, ("dom", "sub")),
        P(None, ("dom", "sub")),
        P(None, ("dom", "sub")),
        P(None, ("dom", "sub")),
        P(None, ("dom", "sub")),
        P(None, ("dom", "sub")),
    )
    out_specs = (P(("dom", "sub"), None), P(("dom", "sub")))
    return jax.shard_map(body, mesh=mesh, in_specs=in_specs, out_specs=out_specs, check_vma=False)
```
